768 devices in a mesh: space: 12 (over z_hi, x), inst: 8 (over y), blade: 8 (over z_lo, core).
Axes of the slice: x: 4, y: 8, z: 12 (z_hi: 3, z_lo: 4; z = z_hi * 4 + z_lo), core: 2. Of those that a mesh axis runs over, the one named last changes fastest.
Arguments:
- state: bfloat16 [8, 16, 5, 96, 1024], P('blade', 'inst', None, 'space'), may hold values from -6 to 6
- flux_x: float32 [5, 5], replicated, may hold values from -2.5 to 2.5
- flux_c: float32 [5, 5], replicated, may hold values from -2.5 to 2.5
- pressure_weights: float32 [5], replicated, may hold values from 0.2 to 1
- coupling: float32 [5], replicated, may hold values from -1.5 to 1.5
- mode_shapes: float32 [8, 64, 3072], P('blade', None, 'space'), may hold values from -6 to 6
- stiffness: float32 [64], replicated, may hold values from 512 to 4096
- surf_index: int32 [8, 3072], P('blade', 'space'), may hold values from 0 to 8191, as said below
- surf_count: int32 [8, 12], P('blade', 'space'), may hold values from 64 to 256, as said below
- blade_of_row: int32 [8, 3072], P('blade', 'space'), may hold values from 0 to 1
- phase_shift: int32 [16], replicated, may hold values from 0 to 15
Outputs:
- residual: float32 [8, 16, 5, 96, 1024], P('blade', 'inst', None, 'space')
The draws below stay inside these ranges and needn't reach their ends.
Inputs may be any that keep to these rules, and one draw needn't show every extreme that they name: `surf_index`: within one block the surface row slots name distinct cells, numbered 0 to 8191. `surf_count`: some block in every draw has all 256 slots live.
All inputs are finite; a program needn't handle non-finite values.
Results may differ from the reference program's by a relative error of at most 0.0003.
Values may be sent and summed in bfloat16 or wider, within the bound.
A program may use at most 32 MiB of HBM per device.

```python
import math
import jax
import jax.numpy as jnp
from jax import lax

COMP = 5
CX = 8
NC = 1024
MODES = 64
ROWS = 256
BPG = 2
NB = 8
NI = 16
NSB = 12
NX = 96
BLADES = 16


def draw_surf_index(key, part):
    keys = jax.random.split(key, NB * NSB)
    picked = jax.vmap(lambda single: jax.random.permutation(single, CX * NC)[:ROWS])(keys)
    return picked.astype(jnp.int32).reshape(NB, NSB * ROWS)


def draw_surf_count(key, part):
    counts = jax.random.randint(jax.random.fold_in(key, 11), (NB * NSB,), ROWS // 4, ROWS + 1)
    fullest = jax.random.randint(jax.random.fold_in(key, 12), (), 0, NB * NSB)
    counts = jnp.where(jnp.arange(NB * NSB) == fullest, ROWS, counts)
    return counts.astype(jnp.int32).reshape(NB, NSB)


def with_ends(entries, rng, least, largest):
    spot = [jax.random.randint(jax.random.fold_in(rng, axis), (), 0, length) for axis, length in enumerate(entries.shape)]
    longest = entries.shape.index(max(entries.shape))
    beside = spot[:longest] + [(spot[longest] + 1) % entries.shape[longest]] + spot[longest + 1:]
    return entries.at[tuple(spot)].set(least).at[tuple(beside)].set(largest)


def block_levels(key, extent, cuts, least, top_value):
    def one(position, parts):
        steps = jax.random.uniform(jax.random.fold_in(jax.random.fold_in(key, 6), position), (parts,), jnp.float32, least / len(cuts), top_value / len(cuts))
        return jnp.repeat(jnp.exp(steps), extent[position] // parts).reshape((-1,) + (1,) * (len(extent) - position - 1))

    gain = one(*cuts[0])
    for cut in cuts[1:]:
        gain = gain * one(*cut)
    return gain


def scatter_about(own_key, extent, spread, bound, cuts=(), kind=jnp.bfloat16):
    array = spread * jax.random.normal(own_key, extent, jnp.float32)
    if cuts:
        array = array * block_levels(own_key, extent, cuts, -0.22, 0.18)
    return jnp.clip(array, -bound, bound).astype(kind)


def setup_inputs(seed: int = 0) -> dict:
    streams_of = jax.random.split(jax.random.key(seed), 12)
    return {
        "state": scatter_about(streams_of[0], (NB, NI, COMP, NX, NC), 1.0, 6.0, ((0, 8), (1, 8), (3, 12))),
        "flux_x": scatter_about(streams_of[1], (COMP, COMP), COMP ** -0.5, 2.5, (), jnp.float32),
        "flux_c": scatter_about(streams_of[2], (COMP, COMP), COMP ** -0.5, 2.5, (), jnp.float32),
        "pressure_weights": jnp.clip(jax.random.uniform(streams_of[3], (COMP,), jnp.float32, 0.2, 1.0), 0.2, 1.0),
        "coupling": jnp.clip(jax.random.uniform(streams_of[4], (COMP,), jnp.float32, -1.5, 1.5), -1.5, 1.5),
        "mode_shapes": scatter_about(streams_of[5], (NB, MODES, NSB * ROWS), 1.0, 6.0, ((0, 8), (2, 12)), jnp.float32),
        "stiffness": jnp.clip(jnp.exp(jax.random.uniform(streams_of[6], (MODES,), jnp.float32, math.log(512.0), math.log(4096.0))), 512.0, 4096.0),
        "surf_index": draw_surf_index(jax.random.fold_in(streams_of[11], 71), 0),
        "surf_count": draw_surf_count(jax.random.fold_in(streams_of[11], 71), 0),
        "blade_of_row": with_ends(jax.random.randint(streams_of[9], (NB, NSB * ROWS), 0, BPG), jax.random.fold_in(streams_of[9], 1), 0, BPG - 1).astype(jnp.int32),
        "phase_shift": with_ends(jax.random.randint(streams_of[10], (BLADES,), 0, NI), jax.random.fold_in(streams_of[10], 1), 0, NI - 1).astype(jnp.int32),
    }


HIGH = lax.Precision.HIGHEST


def spectral_matrix(count):
    first = jnp.arange(count, dtype=jnp.int32)[:, None]
    second = jnp.arange(count, dtype=jnp.int32)[None, :]
    offset = first - second
    apart = offset != 0
    angle = jnp.pi * offset.astype(jnp.float32) / count
    parity = jnp.where(offset % 2 == 0, 1.0, -1.0).astype(jnp.float32)
    safe_sin = jnp.where(apart, jnp.sin(angle), 1.0)
    cotan = jnp.where(apart, 0.5 * parity * jnp.cos(angle) / safe_sin, 0.0)
    return cotan.astype(jnp.float32)


def place(index, values):
    return jnp.zeros((CX * NC,), jnp.float32).at[index].add(values)


def reference(state, flux_x, flux_c, pressure_weights, coupling, mode_shapes, stiffness, surf_index, surf_count, blade_of_row, phase_shift):
    u = state.astype(jnp.float32)
    qmat = spectral_matrix(NI)
    spect = jnp.einsum('ij,bjcxw->bicxw', qmat, u, precision=HIGH)
    padded = jnp.pad(u, ((0, 0), (0, 0), (0, 0), (1, 1), (0, 0)))
    xplus = padded[:, :, :, 2:, :]
    xminus = padded[:, :, :, :-2, :]
    cplus = jnp.roll(u, -1, axis=4)
    cminus = jnp.roll(u, 1, axis=4)
    flow_x = jnp.einsum('kc,bicxw->bikxw', flux_x, xplus - xminus, precision=HIGH)
    flow_c = jnp.einsum('kc,bicxw->bikxw', flux_c, cplus - cminus, precision=HIGH)
    space = 0.5 * flow_x + 0.5 * flow_c - 0.25 * (xplus + xminus + cplus + cminus - 4.0 * u)
    blocks = u.reshape(NB, NI, COMP, NSB, CX, NC).reshape(NB, NI, COMP, NSB, CX * NC)
    pfield = jnp.einsum('k,biksn->bisn', pressure_weights, blocks, precision=HIGH)
    index3 = surf_index.reshape(NB, NSB, ROWS)
    prow = jnp.take_along_axis(pfield, index3[:, None, :, :], axis=3)
    live = jnp.arange(ROWS, dtype=jnp.int32)[None, None, :] < surf_count[:, :, None]
    owner = blade_of_row.reshape(NB, NSB, ROWS)
    onehot = ((owner[..., None] == jnp.arange(BPG, dtype=jnp.int32)) & live[..., None]).astype(jnp.float32)
    phi = mode_shapes.reshape(NB, MODES, NSB, ROWS)
    force = jnp.einsum('bisr,bmsr,bsrq->bimq', prow, phi, onehot, precision=HIGH)
    shifts = phase_shift.reshape(NB, BPG)
    column = (jnp.arange(NI, dtype=jnp.int32)[None, None, :] - shifts[:, :, None]) % NI
    sel = (column[..., None] == jnp.arange(NI, dtype=jnp.int32)).astype(jnp.float32)
    reference_force = jnp.einsum('bimq,bqis->ms', force, sel, precision=HIGH)
    amplitude = reference_force / stiffness[:, None]
    blade_amp = jnp.einsum('ms,bqis->bimq', amplitude, sel, precision=HIGH)
    displacement = jnp.einsum('bmsr,bimq,bsrq->bisr', phi, blade_amp, onehot, precision=HIGH)
    inner = jax.vmap(place, (0, 0))
    middle = jax.vmap(inner, (None, 0))
    dfield = jax.vmap(middle, (0, 0))(index3, displacement)
    dfield = dfield.reshape(NB, NI, NSB, CX, NC).reshape(NB, NI, NX, NC)
    wall = coupling[None, None, :, None, None] * dfield[:, :, None, :, :]
    return spect + space + wall
```

```python
import functools
import math

import jax
import jax.numpy as jnp
from jax import lax
from jax.experimental import pallas as pl
from jax.experimental.pallas import tpu as pltpu
from jax.sharding import PartitionSpec as P

COMP = 5
CX = 8
NC = 1024
MODES = 64
ROWS = 256
BPG = 2
HELD = 2
PLANES = HELD * COMP
DEEP = PLANES * CX
LANES = 128
NB_LANE = NC // LANES
CHUNKS = 4
WIDTH = NC // CHUNKS

HIGH = lax.Precision.HIGHEST
MESH = pl.DeviceIdType.MESH
F32 = jnp.float32


def spectral(offset, count):
    offset %= count
    if offset == 0:
        return 0.0
    angle = math.pi * offset / count
    return 0.5 * (-1.0) ** offset * math.cos(angle) / math.sin(angle)


def dot(a, b, dims):
    return lax.dot_general(a, b, (dims, ((), ())), precision=HIGH, preferred_element_type=F32)


def kernel(
    sizes,
    state,
    fx,
    fc,
    pw,
    cpl,
    modes,
    stiff,
    index,
    count,
    owner,
    shift,
    out,
    mine,
    phi,
    dcs,
    fromleft,
    fromright,
    hrow,
    hsend,
    hrecv,
    pf,
    dsc,
    part,
    box0,
    box1,
    box2,
    load_sem,
    sl_sem,
    rl_sem,
    sr_sem,
    rr_sem,
    hs_sem,
    hr_sem,
    as_sem,
    ar_sem,
):
    n_space, n_inst, n_blade = sizes
    half = n_inst // 2
    ninst = n_inst * HELD
    my_space = lax.axis_index("space")
    my_inst = lax.axis_index("inst")
    my_blade = lax.axis_index("blade")

    loads = [
        pltpu.make_async_copy(state, mine, load_sem.at[0]),
        pltpu.make_async_copy(modes, phi.at[pl.ds(0, MODES)], load_sem.at[1]),
        pltpu.make_async_copy(modes, phi.at[pl.ds(MODES, MODES)], load_sem.at[2]),
    ]
    for copy in loads:
        copy.start()

    stages = (("space", n_space, my_space, box0), ("blade", n_blade, my_blade, box1), ("inst", n_inst, my_inst, box2))
    barrier = pltpu.get_barrier_semaphore()
    for axis, size, me, _ in stages:
        for k in range(1, size):
            pl.semaphore_signal(barrier, inc=1, device_id={axis: lax.rem(me + k, size)}, device_id_type=MESH)
    pl.semaphore_wait(barrier, n_space + n_inst + n_blade - 3)

    right = lax.rem(my_inst + 1, n_inst)
    left = lax.rem(my_inst + n_inst - 1, n_inst)

    def columns(chunk):
        return pl.ds(chunk * WIDTH, WIDTH)

    def to_right(hop, chunk):
        src = mine if hop == 1 else fromleft.at[hop - 2]
        return pltpu.make_async_remote_copy(
            src_ref=src.at[:, columns(chunk)],
            dst_ref=fromleft.at[hop - 1, :, columns(chunk)],
            send_sem=sr_sem.at[hop - 1, chunk],
            recv_sem=rl_sem.at[hop - 1, chunk],
            device_id={"inst": right},
            device_id_type=MESH,
        )

    def to_left(hop, chunk):
        src = mine if hop == 1 else fromright.at[hop - 2]
        return pltpu.make_async_remote_copy(
            src_ref=src.at[:, columns(chunk)],
            dst_ref=fromright.at[hop - 1, :, columns(chunk)],
            send_sem=sl_sem.at[hop - 1, chunk],
            recv_sem=rr_sem.at[hop - 1, chunk],
            device_id={"inst": left},
            device_id_type=MESH,
        )

    def going(hop):
        rights = [c for c in range(CHUNKS) if hop < half or c < CHUNKS // 2]
        lefts = [c for c in reversed(range(CHUNKS)) if hop < half or c >= CHUNKS // 2]
        return list(zip(rights, lefts))

    loads[0].wait()
    for c_right, c_left in going(1):
        to_right(1, c_right).start()
        to_left(1, c_left).start()

    def block(ref, lanes):
        got = []
        for group in range(DEEP // 16):
            pair = ref[pl.ds(16 * group, 16), lanes].astype(F32)
            got += [pair[0:CX], pair[CX : 2 * CX]]
        return got

    def lane_block(j):
        return pl.ds(pl.multiple_of(j * LANES, LANES), LANES)

    def pressure(j, carry):
        planes = block(mine, lane_block(j))
        for i in range(HELD):
            total = pw[0] * planes[i * COMP]
            for k in range(1, COMP):
                total = total + pw[k] * planes[i * COMP + k]
            pf[pl.ds(pl.multiple_of(j * CX, CX), CX), pl.ds(i * LANES, LANES)] = total
        return carry

    lax.fori_loop(0, NB_LANE, pressure, 0)

    cell = index[...]
    high = ((cell >> 7) & 7) * CX + (cell >> 10)
    low = cell & (LANES - 1)
    at_high = (lax.broadcasted_iota(jnp.int32, (CX * NB_LANE, ROWS), 0) == high).astype(F32)
    at_low = lax.broadcasted_iota(jnp.int32, (LANES, ROWS), 0) == low
    live = lax.broadcasted_iota(jnp.int32, (1, ROWS), 1) < count[0, 0]
    lag = jnp.where(owner[...] == 0, shift[my_blade * BPG], shift[my_blade * BPG + 1])
    slot = lax.broadcasted_iota(jnp.int32, (ninst, ROWS), 0)
    picks = [(((my_inst * HELD + i - lag) & (ninst - 1)) == slot) & live for i in range(HELD)]

    rows = dot(pf[...], at_high, ((0,), (0,)))
    placed = jnp.zeros((ninst, ROWS), F32)
    for i in range(HELD):
        prow = jnp.sum(jnp.where(at_low, rows[i * LANES : (i + 1) * LANES], 0.0), axis=0, keepdims=True)
        placed = placed + jnp.where(picks[i], prow, 0.0)
    loads[1].wait()
    loads[2].wait()
    force = dot(placed, phi[...], ((1,), (1,)))
    first_half = lax.broadcasted_iota(jnp.int32, (CX, LANES), 1) < MODES
    part[0] = jnp.where(first_half, force[0:CX], force[CX : 2 * CX])

    def send_part(s):
        axis, size, me, box = stages[s]
        for k in range(1, size):
            pltpu.make_async_remote_copy(
                src_ref=part.at[s],
                dst_ref=box.at[k - 1],
                send_sem=as_sem.at[s],
                recv_sem=ar_sem.at[s],
                device_id={axis: lax.rem(me + k, size)},
                device_id_type=MESH,
            ).start()

    def sum_part(s):
        size, box = stages[s][1], stages[s][3]
        pltpu.make_async_copy(box, box, ar_sem.at[s]).wait()
        total = part[s]
        for k in range(size - 1):
            total = total + box[k]
        return total

    send_part(0)

    hrow[...] = jnp.zeros_like(hrow)
    for group in range(DEEP // 16):
        pair = mine[pl.ds(16 * group, 16), :].astype(F32)
        for odd in range(2):
            plane = 2 * group + odd
            hrow[0, pl.ds(plane, 1), :] = pair[odd * CX : odd * CX + 1]
            hrow[1, pl.ds(plane, 1), :] = pair[odd * CX + CX - 1 : odd * CX + CX]
    for side in range(2):
        hsend[side] = hrow[side].astype(jnp.bfloat16)
    halos = []
    for side, step in ((0, n_space - 1), (1, 1)):
        halos.append(
            pltpu.make_async_remote_copy(
                src_ref=hsend.at[side],
                dst_ref=hrecv.at[side],
                send_sem=hs_sem.at[side],
                recv_sem=hr_sem.at[side],
                device_id={"space": lax.rem(my_space + step, n_space)},
                device_id_type=MESH,
            )
        )
        halos[-1].start()

    for group in range(DEEP // 16):
        pair = mine[pl.ds(16 * group, 16), :].astype(F32)
        ahead = pltpu.roll(pair, NC - 1, 1)
        behind = pltpu.roll(pair, 1, 1)
        dcs[pl.ds(16 * group, 16), :] = ahead - behind
        out[pl.ds(16 * group, 16), :] = pair - 0.25 * (ahead + behind)

    for copy in halos:
        copy.wait_recv()
    nexts = hrecv[0].astype(F32) * jnp.where(my_space == n_space - 1, 0.0, 1.0)
    hrow[0] = nexts
    hrow[1] = hrecv[1].astype(F32) * jnp.where(my_space == 0, 0.0, 1.0)

    layer = lax.broadcasted_iota(jnp.int32, (CX, LANES), 0)

    def local(j, carry):
        lanes = lane_block(j)
        planes = block(mine, lanes)
        for i in range(HELD):
            dx, dc = [], []
            for k in range(COMP):
                p = i * COMP + k
                up = jnp.where(layer == CX - 1, hrow[0, pl.ds(p, 1), lanes], pltpu.roll(planes[p], CX - 1, 0))
                down = jnp.where(layer == 0, hrow[1, pl.ds(p, 1), lanes], pltpu.roll(planes[p], 1, 0))
                dx.append(up - down)
                dc.append(dcs[pl.ds(p * CX, CX), lanes])
                at = pl.ds(p * CX, CX)
                value = out[at, lanes] - 0.25 * (up + down)
                for r in range(HELD):
                    value = value + spectral(i - r, ninst) * planes[r * COMP + k]
                out[at, lanes] = value
            for k in range(COMP):
                at = pl.ds((i * COMP + k) * CX, CX)
                flow = fx[k, 0] * dx[0] + fc[k, 0] * dc[0]
                for c in range(1, COMP):
                    flow = flow + fx[k, c] * dx[c] + fc[k, c] * dc[c]
                out[at, lanes] = out[at, lanes] + 0.5 * flow
        return carry

    lax.fori_loop(0, NB_LANE, local, 0)

    def add_blocks(sources, first, last):
        def add(j, carry):
            lanes = lane_block(j)
            sums = [out[pl.ds(p * CX, CX), lanes] for p in range(PLANES)]
            for ref, offset in sources:
                planes = block(ref, lanes)
                for i in range(HELD):
                    for k in range(COMP):
                        for r in range(HELD):
                            sums[i * COMP + k] += spectral(HELD * offset + i - r, ninst) * planes[r * COMP + k]
            for p in range(PLANES):
                out[pl.ds(p * CX, CX), lanes] = sums[p]
            return carry

        lax.fori_loop(first, last, add, 0)

    for hop in range(1, half + 1):
        onward = going(hop + 1) if hop < half else []
        for pair in going(hop):
            to_right(hop, pair[0]).wait_recv()
            if pair[0] in [c for c, _ in onward]:
                to_right(hop + 1, pair[0]).start()
            to_left(hop, pair[1]).wait_recv()
            if pair[1] in [c for _, c in onward]:
                to_left(hop + 1, pair[1]).start()
        if hop == 1:
            part[1] = sum_part(0)
            send_part(1)
        if hop == 2:
            part[2] = sum_part(1)
            send_part(2)
        if hop == 3:
            total = sum_part(2)
            rigid = jnp.concatenate([stiff[...], stiff[...]], axis=1)
            amp = total / rigid
            both = jnp.concatenate([jnp.where(first_half, amp, 0.0), jnp.where(first_half, 0.0, amp)], axis=0)
            moved = dot(both, phi[...], ((1,), (0,)))
            spread = []
            for i in range(HELD):
                disp = jnp.sum(jnp.where(picks[i], moved, 0.0), axis=0, keepdims=True)
                spread.append(jnp.where(at_low, disp, 0.0))
            dsc[...] = dot(at_high, jnp.concatenate(spread, axis=0), ((1,), (1,)))

            def wall(j, carry):
                lanes = lane_block(j)
                for i in range(HELD):
                    field = dsc[pl.ds(pl.multiple_of(j * CX, CX), CX), pl.ds(i * LANES, LANES)]
                    for k in range(COMP):
                        at = pl.ds((i * COMP + k) * CX, CX)
                        out[at, lanes] = out[at, lanes] + cpl[k] * field
                return carry

            lax.fori_loop(0, NB_LANE, wall, 0)
        if hop < half:
            add_blocks([(fromleft.at[hop - 1], hop), (fromright.at[hop - 1], -hop)], 0, NB_LANE)
        else:
            add_blocks([(fromleft.at[hop - 1], hop)], 0, NB_LANE // 2)
            add_blocks([(fromright.at[hop - 1], -hop)], NB_LANE // 2, NB_LANE)

    for hop in range(1, half + 1):
        for c_right, c_left in going(hop):
            to_right(hop, c_right).wait_send()
            to_left(hop, c_left).wait_send()
    for copy in halos:
        copy.wait_send()
    for s in range(3):
        box = stages[s][3]
        pltpu.make_async_copy(box, box, as_sem.at[s]).wait()


def body(sizes, state, fx, fc, pw, cpl, modes, stiff, index, count, owner, shift):
    n_space, n_inst, n_blade = sizes
    half = n_inst // 2
    smem = pl.BlockSpec(memory_space=pltpu.SMEM)
    vmem = pl.BlockSpec(memory_space=pltpu.VMEM)
    hbm = pl.BlockSpec(memory_space=pl.ANY)
    dma = pltpu.SemaphoreType.DMA
    out = pl.pallas_call(
        functools.partial(kernel, sizes),
        out_shape=jax.ShapeDtypeStruct((DEEP, NC), F32),
        in_specs=[hbm, smem, smem, smem, smem, hbm, vmem, vmem, smem, vmem, smem],
        out_specs=vmem,
        scratch_shapes=[
            pltpu.VMEM((DEEP, NC), jnp.bfloat16),
            pltpu.VMEM((2 * MODES, ROWS), F32),
            pltpu.VMEM((DEEP, NC), F32),
            pltpu.VMEM((half, DEEP, NC), jnp.bfloat16),
            pltpu.VMEM((half, DEEP, NC), jnp.bfloat16),
            pltpu.VMEM((2, 16, NC), F32),
            pltpu.VMEM((2, 16, NC), jnp.bfloat16),
            pltpu.VMEM((2, 16, NC), jnp.bfloat16),
            pltpu.VMEM((CX * NB_LANE, HELD * LANES), F32),
            pltpu.VMEM((CX * NB_LANE, HELD * LANES), F32),
            pltpu.VMEM((3, CX, LANES), F32),
            pltpu.VMEM((n_space - 1, CX, LANES), F32),
            pltpu.VMEM((n_blade - 1, CX, LANES), F32),
            pltpu.VMEM((n_inst - 1, CX, LANES), F32),
            dma((3,)),
            dma((half, CHUNKS)),
            dma((half, CHUNKS)),
            dma((half, CHUNKS)),
            dma((half, CHUNKS)),
            dma((2,)),
            dma((2,)),
            dma((3,)),
            dma((3,)),
        ],
        compiler_params=pltpu.CompilerParams(
            collective_id=0, has_side_effects=True, vmem_limit_bytes=24 * 1024 * 1024
        ),
        name="residual",
    )(
        state.reshape(DEEP, NC),
        fx,
        fc,
        pw,
        cpl,
        modes.reshape(MODES, ROWS),
        stiff.reshape(1, MODES),
        index,
        count,
        owner,
        shift,
    )
    return out.reshape(1, HELD, COMP, CX, NC)


def solution(mesh):
    sizes = (mesh.shape["space"], mesh.shape["inst"], mesh.shape["blade"])
    placed = (
        P("blade", "inst", None, "space", None),
        P(),
        P(),
        P(),
        P(),
        P("blade", None, "space"),
        P(),
        P("blade", "space"),
        P("blade", "space"),
        P("blade", "space"),
        P(),
    )
    return jax.shard_map(
        functools.partial(body, sizes),
        mesh=mesh,
        in_specs=placed,
        out_specs=P("blade", "inst", None, "space", None),
        check_vma=False,
    )
```

```python
import functools
import itertools
import math

import jax
import jax.numpy as jnp
from jax import lax
from jax.experimental import pallas as pl
from jax.experimental.pallas import tpu as pltpu
from jax.sharding import PartitionSpec as P

COMP = 5
CX = 8
NC = 1024
MODES = 64
ROWS = 256
BPG = 2
HELD = 2
PLANES = HELD * COMP
DEEP = PLANES * CX
LANES = 128
NB_LANE = NC // LANES
CHUNKS = 4
WIDTH = NC // CHUNKS
STAGES = (("x", "y"), ("zhi", "zlo", "core"))

HIGH = lax.Precision.HIGHEST
MESH = pl.DeviceIdType.MESH
F32 = jnp.float32


def spectral(offset, count):
    offset %= count
    if offset == 0:
        return 0.0
    angle = math.pi * offset / count
    return 0.5 * (-1.0) ** offset * math.cos(angle) / math.sin(angle)


def dot(a, b, dims):
    return lax.dot_general(a, b, (dims, ((), ())), precision=HIGH, preferred_element_type=F32)


SUB = {"zhi": 3, "x": 4, "y": 8, "zlo": 4, "core": 2}


def sub_index(at):
    return {
        "zhi": at["space"] // SUB["x"],
        "x": lax.rem(at["space"], SUB["x"]),
        "y": at["inst"],
        "zlo": at["blade"] // SUB["core"],
        "core": lax.rem(at["blade"], SUB["core"]),
    }


def mesh_index(sub):
    return {
        "space": sub["zhi"] * SUB["x"] + sub["x"],
        "inst": sub["y"],
        "blade": sub["zlo"] * SUB["core"] + sub["core"],
    }


def exchange_stages(sizes):
    assert sizes == (SUB["zhi"] * SUB["x"], SUB["y"], SUB["zlo"] * SUB["core"])

    def around(offset, size):
        return min(offset, size - offset)

    def hops(o):
        return around(o["x"], 4) + around(o["y"], 8) + around((4 * o["zhi"] + o["zlo"]) % 12, 12) + 0.5 * o["core"]

    stages = []
    for axes in STAGES:
        ranges = [range(SUB[a]) if a in axes else (0,) for a in SUB]
        offsets = [dict(zip(SUB, o)) for o in itertools.product(*ranges) if any(o)]
        stages.append(sorted(offsets, key=lambda o: -hops(o)))
    return stages


def kernel(
    sizes,
    count,
    state_hbm,
    fx_hbm,
    fc_hbm,
    pw_hbm,
    cpl_hbm,
    modes_hbm,
    stiff_hbm,
    index_hbm,
    owner_hbm,
    shift_hbm,
    out,
    field,
    gain,
    mine,
    phi,
    fx,
    fc,
    pw,
    stiff,
    index,
    owner,
    shift,
    dcs,
    fromleft,
    fromright,
    hrow,
    hsend,
    hrecv,
    pf,
    part,
    box0,
    box1,
    load_sem,
    sl_sem,
    rl_sem,
    sr_sem,
    rr_sem,
    hs_sem,
    hr_sem,
    as_sem,
    ar_sem,
):
    n_space, n_inst, n_blade = sizes
    half = n_inst // 2
    ninst = n_inst * HELD
    my_space = lax.axis_index("space")
    my_inst = lax.axis_index("inst")
    my_blade = lax.axis_index("blade")

    moves = (
        (state_hbm, mine),
        (index_hbm, index),
        (pw_hbm, pw),
        (owner_hbm, owner),
        (shift_hbm, shift),
        (modes_hbm, phi.at[pl.ds(0, MODES)]),
        (modes_hbm, phi.at[pl.ds(MODES, MODES)]),
        (fx_hbm, fx),
        (fc_hbm, fc),
        (stiff_hbm, stiff),
        (cpl_hbm, gain),
    )
    loads = [pltpu.make_async_copy(src, dst, load_sem.at[n]) for n, (src, dst) in enumerate(moves)]
    for copy in loads:
        copy.start()

    stages = exchange_stages(sizes)
    mesh_at = {"space": my_space, "inst": my_inst, "blade": my_blade}
    my_sub = sub_index(mesh_at)

    def peer(offsets):
        return mesh_index({a: lax.rem(my_sub[a] + offsets[a], SUB[a]) if offsets[a] else my_sub[a] for a in SUB})

    right = lax.rem(my_inst + 1, n_inst)
    left = lax.rem(my_inst + n_inst - 1, n_inst)
    following = lax.rem(my_space + 1, n_space)
    preceding = lax.rem(my_space + n_space - 1, n_space)

    barrier = pltpu.get_barrier_semaphore()
    greeted = [peer(o) for stage in stages for o in stage]
    greeted += [{"space": following}, {"space": preceding}]
    for other in greeted:
        pl.semaphore_signal(barrier, inc=1, device_id=other, device_id_type=MESH)

    def columns(chunk):
        return pl.ds(chunk * WIDTH, WIDTH)

    def to_right(hop, chunk):
        src = mine if hop == 1 else fromleft.at[hop - 2]
        return pltpu.make_async_remote_copy(
            src_ref=src.at[:, columns(chunk)],
            dst_ref=fromleft.at[hop - 1, :, columns(chunk)],
            send_sem=sr_sem.at[hop - 1, chunk],
            recv_sem=rl_sem.at[hop - 1, chunk],
            device_id={"inst": right},
            device_id_type=MESH,
        )

    def to_left(hop, chunk):
        src = mine if hop == 1 else fromright.at[hop - 2]
        return pltpu.make_async_remote_copy(
            src_ref=src.at[:, columns(chunk)],
            dst_ref=fromright.at[hop - 1, :, columns(chunk)],
            send_sem=sl_sem.at[hop - 1, chunk],
            recv_sem=rr_sem.at[hop - 1, chunk],
            device_id={"inst": left},
            device_id_type=MESH,
        )

    def going(hop):
        rights = [c for c in range(CHUNKS) if hop < half or c < CHUNKS // 2]
        lefts = [c for c in reversed(range(CHUNKS)) if hop < half or c >= CHUNKS // 2]
        return list(zip(rights, lefts))

    def block(ref, lanes):
        got = []
        for group in range(DEEP // 16):
            pair = ref[pl.ds(16 * group, 16), lanes].astype(F32)
            got += [pair[0:CX], pair[CX : 2 * CX]]
        return got

    def lane_block(j):
        return pl.ds(pl.multiple_of(j * LANES, LANES), LANES)

    for copy in loads[0:5]:
        copy.wait()

    def pressure(j, carry):
        planes = block(mine, lane_block(j))
        for i in range(HELD):
            total = pw[0] * planes[i * COMP]
            for k in range(1, COMP):
                total = total + pw[k] * planes[i * COMP + k]
            pf[pl.ds(pl.multiple_of(j * CX, CX), CX), pl.ds(i * LANES, LANES)] = total
        return carry

    lax.fori_loop(0, NB_LANE, pressure, 0)

    cell = index[...]
    high = ((cell >> 7) & 7) * CX + (cell >> 10)
    low = cell & (LANES - 1)
    at_high = (lax.broadcasted_iota(jnp.int32, (CX * NB_LANE, ROWS), 0) == high).astype(F32)
    at_low = lax.broadcasted_iota(jnp.int32, (LANES, ROWS), 0) == low
    live = lax.broadcasted_iota(jnp.int32, (1, ROWS), 1) < count[0, 0]
    lag = jnp.where(owner[...] == 0, shift[my_blade * BPG], shift[my_blade * BPG + 1])
    slot = lax.broadcasted_iota(jnp.int32, (ninst, ROWS), 0)
    picks = [(((my_inst * HELD + i - lag) & (ninst - 1)) == slot) & live for i in range(HELD)]

    rows = dot(pf[...], at_high, ((0,), (0,)))
    placed = jnp.zeros((ninst, ROWS), F32)
    for i in range(HELD):
        prow = jnp.sum(jnp.where(at_low, rows[i * LANES : (i + 1) * LANES], 0.0), axis=0, keepdims=True)
        placed = placed + jnp.where(picks[i], prow, 0.0)
    for copy in loads[5:7]:
        copy.wait()
    force = dot(placed, phi[...], ((1,), (1,)))
    first_half = lax.broadcasted_iota(jnp.int32, (CX, LANES), 1) < MODES
    part[0] = jnp.where(first_half, force[0:CX], force[CX : 2 * CX])

    boxes = (box0, box1)

    def send_part(s):
        for k, offsets in enumerate(stages[s]):
            pltpu.make_async_remote_copy(
                src_ref=part.at[s],
                dst_ref=boxes[s].at[k],
                send_sem=as_sem.at[s],
                recv_sem=ar_sem.at[s],
                device_id=peer(offsets),
                device_id_type=MESH,
            ).start()

    def sum_part(s):
        box = boxes[s]
        pltpu.make_async_copy(box, box, ar_sem.at[s]).wait()
        total = part[s]
        for k in range(len(stages[s])):
            total = total + box[k]
        return total

    pl.semaphore_wait(barrier, len(greeted))
    send_part(0)

    for c_right, c_left in going(1):
        to_right(1, c_right).start()
        to_left(1, c_left).start()

    hrow[...] = jnp.zeros_like(hrow)
    for group in range(DEEP // 16):
        pair = mine[pl.ds(16 * group, 16), :].astype(F32)
        for odd in range(2):
            plane = 2 * group + odd
            hrow[0, pl.ds(plane, 1), :] = pair[odd * CX : odd * CX + 1]
            hrow[1, pl.ds(plane, 1), :] = pair[odd * CX + CX - 1 : odd * CX + CX]
    for side in range(2):
        hsend[side] = hrow[side].astype(jnp.bfloat16)
    halos = []
    for side, other in ((0, preceding), (1, following)):
        halos.append(
            pltpu.make_async_remote_copy(
                src_ref=hsend.at[side],
                dst_ref=hrecv.at[side],
                send_sem=hs_sem.at[side],
                recv_sem=hr_sem.at[side],
                device_id={"space": other},
                device_id_type=MESH,
            )
        )
        halos[-1].start()

    for group in range(DEEP // 16):
        pair = mine[pl.ds(16 * group, 16), :].astype(F32)
        ahead = pltpu.roll(pair, NC - 1, 1)
        behind = pltpu.roll(pair, 1, 1)
        dcs[pl.ds(16 * group, 16), :] = ahead - behind
        out[pl.ds(16 * group, 16), :] = pair - 0.25 * (ahead + behind)

    part[1] = sum_part(0)
    send_part(1)

    for copy in loads[7:]:
        copy.wait()
    for copy in halos:
        copy.wait_recv()
    hrow[0] = hrecv[0].astype(F32) * jnp.where(my_space == n_space - 1, 0.0, 1.0)
    hrow[1] = hrecv[1].astype(F32) * jnp.where(my_space == 0, 0.0, 1.0)

    layer = lax.broadcasted_iota(jnp.int32, (CX, LANES), 0)

    def local(j, carry):
        lanes = lane_block(j)
        planes = block(mine, lanes)
        for i in range(HELD):
            dx, dc = [], []
            for k in range(COMP):
                p = i * COMP + k
                up = jnp.where(layer == CX - 1, hrow[0, pl.ds(p, 1), lanes], pltpu.roll(planes[p], CX - 1, 0))
                down = jnp.where(layer == 0, hrow[1, pl.ds(p, 1), lanes], pltpu.roll(planes[p], 1, 0))
                dx.append(up - down)
                dc.append(dcs[pl.ds(p * CX, CX), lanes])
                at = pl.ds(p * CX, CX)
                value = out[at, lanes] - 0.25 * (up + down)
                for r in range(HELD):
                    value = value + spectral(i - r, ninst) * planes[r * COMP + k]
                out[at, lanes] = value
            for k in range(COMP):
                at = pl.ds((i * COMP + k) * CX, CX)
                flow = fx[k, 0] * dx[0] + fc[k, 0] * dc[0]
                for c in range(1, COMP):
                    flow = flow + fx[k, c] * dx[c] + fc[k, c] * dc[c]
                out[at, lanes] = out[at, lanes] + 0.5 * flow
        return carry

    def add_blocks(sources, first, last):
        def add(j, carry):
            lanes = lane_block(j)
            sums = [out[pl.ds(p * CX, CX), lanes] for p in range(PLANES)]
            for ref, offset in sources:
                planes = block(ref, lanes)
                for i in range(HELD):
                    for k in range(COMP):
                        for r in range(HELD):
                            sums[i * COMP + k] += spectral(HELD * offset + i - r, ninst) * planes[r * COMP + k]
            for p in range(PLANES):
                out[pl.ds(p * CX, CX), lanes] = sums[p]
            return carry

        lax.fori_loop(first, last, add, 0)

    for hop in range(1, half + 1):
        onward = going(hop + 1) if hop < half else []
        for pair in going(hop):
            to_right(hop, pair[0]).wait_recv()
            if pair[0] in [c for c, _ in onward]:
                to_right(hop + 1, pair[0]).start()
            to_left(hop, pair[1]).wait_recv()
            if pair[1] in [c for _, c in onward]:
                to_left(hop + 1, pair[1]).start()
        if hop == 1:
            lax.fori_loop(0, NB_LANE, local, 0)
        if hop < half:
            add_blocks([(fromleft.at[hop - 1], hop), (fromright.at[hop - 1], -hop)], 0, NB_LANE)
        else:
            add_blocks([(fromleft.at[hop - 1], hop)], 0, NB_LANE // 2)
            add_blocks([(fromright.at[hop - 1], -hop)], NB_LANE // 2, NB_LANE)

    total = sum_part(1)
    rigid = jnp.concatenate([stiff[...], stiff[...]], axis=1)
    amp = total / rigid
    both = jnp.concatenate([jnp.where(first_half, amp, 0.0), jnp.where(first_half, 0.0, amp)], axis=0)
    moved = dot(both, phi[...], ((1,), (0,)))
    spread = []
    for i in range(HELD):
        disp = jnp.sum(jnp.where(picks[i], moved, 0.0), axis=0, keepdims=True)
        spread.append(jnp.where(at_low, disp, 0.0))
    hit = dot(at_high, jnp.concatenate(spread, axis=0), ((1,), (1,)))
    for i in range(HELD):
        for j in range(NB_LANE):
            field[pl.ds(i * CX, CX), pl.ds(j * LANES, LANES)] = hit[j * CX : (j + 1) * CX, i * LANES : (i + 1) * LANES]

    for hop in range(1, half + 1):
        for c_right, c_left in going(hop):
            to_right(hop, c_right).wait_send()
            to_left(hop, c_left).wait_send()
    for copy in halos:
        copy.wait_send()
    for s in range(2):
        pltpu.make_async_copy(boxes[s], boxes[s], as_sem.at[s]).wait()


def body(sizes, state, fx, fc, pw, cpl, modes, stiff, index, count, owner, shift):
    n_space, n_inst, n_blade = sizes
    half = n_inst // 2
    stages = exchange_stages(sizes)
    vmem = pl.BlockSpec(memory_space=pltpu.VMEM)
    hbm = pl.BlockSpec(memory_space=pltpu.HBM)
    dma = pltpu.SemaphoreType.DMA
    operands = (
        state.reshape(DEEP, NC),
        fx,
        fc,
        pw,
        cpl,
        modes.reshape(MODES, ROWS),
        stiff.reshape(1, MODES),
        index,
        owner,
        shift,
    )
    out, field, gain = pl.pallas_call(
        functools.partial(kernel, sizes),
        out_shape=(jax.ShapeDtypeStruct((DEEP, NC), F32), jax.ShapeDtypeStruct((HELD * CX, NC), F32), jax.ShapeDtypeStruct((COMP,), F32)),
        in_specs=[pl.BlockSpec(memory_space=pltpu.SMEM)] + [hbm] * len(operands),
        out_specs=(vmem, vmem, vmem),
        scratch_shapes=[
            pltpu.VMEM((DEEP, NC), jnp.bfloat16),
            pltpu.VMEM((2 * MODES, ROWS), F32),
            pltpu.SMEM((COMP, COMP), F32),
            pltpu.SMEM((COMP, COMP), F32),
            pltpu.SMEM((COMP,), F32),
            pltpu.VMEM((1, MODES), F32),
            pltpu.VMEM((1, ROWS), jnp.int32),
            pltpu.VMEM((1, ROWS), jnp.int32),
            pltpu.SMEM((n_blade * BPG,), jnp.int32),
            pltpu.VMEM((DEEP, NC), F32),
            pltpu.VMEM((half, DEEP, NC), jnp.bfloat16),
            pltpu.VMEM((half, DEEP, NC), jnp.bfloat16),
            pltpu.VMEM((2, 16, NC), F32),
            pltpu.VMEM((2, 16, NC), jnp.bfloat16),
            pltpu.VMEM((2, 16, NC), jnp.bfloat16),
            pltpu.VMEM((CX * NB_LANE, HELD * LANES), F32),
            pltpu.VMEM((2, CX, LANES), F32),
            pltpu.VMEM((len(stages[0]), CX, LANES), F32),
            pltpu.VMEM((len(stages[1]), CX, LANES), F32),
            dma((len(operands) + 1,)),
            dma((half, CHUNKS)),
            dma((half, CHUNKS)),
            dma((half, CHUNKS)),
            dma((half, CHUNKS)),
            dma((2,)),
            dma((2,)),
            dma((2,)),
            dma((2,)),
        ],
        compiler_params=pltpu.CompilerParams(
            collective_id=0, has_side_effects=True, vmem_limit_bytes=24 * 1024 * 1024
        ),
        name="residual",
    )(count, *[pltpu.with_memory_space_constraint(operand, pltpu.HBM) for operand in operands])
    wall = gain[None, :, None, None] * field.reshape(HELD, 1, CX, NC)
    return (out.reshape(HELD, COMP, CX, NC) + wall)[None]


def solution(mesh):
    sizes = (mesh.shape["space"], mesh.shape["inst"], mesh.shape["blade"])
    placed = (
        P("blade", "inst", None, "space", None),
        P(),
        P(),
        P(),
        P(),
        P("blade", None, "space"),
        P(),
        P("blade", "space"),
        P("blade", "space"),
        P("blade", "space"),
        P(),
    )
    return jax.shard_map(
        functools.partial(body, sizes),
        mesh=mesh,
        in_specs=placed,
        out_specs=P("blade", "inst", None, "space", None),
        check_vma=False,
    )
```

```python
import functools
import itertools
import math

import jax
import jax.numpy as jnp
from jax import lax
from jax.experimental import pallas as pl
from jax.experimental.pallas import tpu as pltpu
from jax.sharding import PartitionSpec as P

COMP = 5
CX = 8
NC = 1024
MODES = 64
ROWS = 256
BPG = 2
HELD = 2
PLANES = HELD * COMP
DEEP = PLANES * CX
LANES = 128
NB_LANE = NC // LANES
CHUNKS = 4
WIDTH = NC // CHUNKS


HIGH = lax.Precision.HIGHEST
MESH = pl.DeviceIdType.MESH
LOGICAL = pl.DeviceIdType.LOGICAL
F32 = jnp.float32


def spectral(offset, count):
    offset %= count
    if offset == 0:
        return 0.0
    angle = math.pi * offset / count
    return 0.5 * (-1.0) ** offset * math.cos(angle) / math.sin(angle)


def dot(a, b, dims):
    return lax.dot_general(a, b, (dims, ((), ())), precision=HIGH, preferred_element_type=F32)


SUB = {"zhi": 3, "x": 4, "y": 8, "zlo": 4, "core": 2}


STEP = {"core": 1, "zlo": 2, "y": 8, "x": 64, "zhi": 256}


def around(offset, size):
    return min(offset, size - offset)


LINE = list(itertools.product(range(SUB["zlo"]), range(SUB["core"])))
PLANE = sorted(
    (o for o in itertools.product(range(SUB["x"]), range(SUB["y"])) if any(o)),
    key=lambda o: -around(o[0], SUB["x"]) - around(o[1], SUB["y"]),
)
FOLLOW = SUB["zhi"] - 1


def place(space, inst, blade):
    here = {
        "zhi": space // SUB["x"],
        "x": space % SUB["x"],
        "y": inst,
        "zlo": blade // SUB["core"],
        "core": blade % SUB["core"],
    }
    table = {}
    for axis, size in SUB.items():
        table[axis] = []
        for offset in range(size):
            at = here[axis] + offset
            table[axis].append(jnp.where(at >= size, at - size, at) * STEP[axis])
    return here, table


def kernel(
    sizes,
    count,
    state_hbm,
    fx_hbm,
    fc_hbm,
    pw_hbm,
    cpl_hbm,
    modes_hbm,
    stiff_hbm,
    index_hbm,
    owner_hbm,
    shift_hbm,
    out,
    field,
    gain,
    mine,
    phi,
    fx,
    fc,
    pw,
    stiff,
    index,
    owner,
    shift,
    dcs,
    fromleft,
    fromright,
    hrow,
    hsend,
    hrecv,
    pf,
    part,
    box0,
    box1,
    whole,
    load_sem,
    sl_sem,
    rl_sem,
    sr_sem,
    rr_sem,
    hs_sem,
    hr_sem,
    as_sem,
    ar_sem,
):
    n_space, n_inst, n_blade = sizes
    half = n_inst // 2
    ninst = n_inst * HELD
    my_space = lax.axis_index("space")
    my_inst = lax.axis_index("inst")
    my_blade = lax.axis_index("blade")

    moves = (
        (state_hbm, mine),
        (index_hbm, index),
        (pw_hbm, pw),
        (owner_hbm, owner),
        (shift_hbm, shift),
        (modes_hbm, phi.at[pl.ds(0, MODES)]),
        (modes_hbm, phi.at[pl.ds(MODES, MODES)]),
        (fx_hbm, fx),
        (fc_hbm, fc),
        (stiff_hbm, stiff),
        (cpl_hbm, gain),
    )
    loads = [pltpu.make_async_copy(src, dst, load_sem.at[n]) for n, (src, dst) in enumerate(moves)]
    for copy in loads:
        copy.start()

    here, table = place(my_space, my_inst, my_blade)
    column = table["x"][0] + table["y"][0]
    stack = table["zlo"][0] + table["core"][0]
    collects = here["zhi"] == 0

    def on_line(zhi, offsets):
        return column + zhi * STEP["zhi"] + table["zlo"][offsets[0]] + table["core"][offsets[1]]

    def on_plane(offsets):
        return stack + table["x"][offsets[0]] + table["y"][offsets[1]]

    right = lax.rem(my_inst + 1, n_inst)
    left = lax.rem(my_inst + n_inst - 1, n_inst)
    following = lax.rem(my_space + 1, n_space)
    preceding = lax.rem(my_space + n_space - 1, n_space)

    barrier = pltpu.get_barrier_semaphore()

    def greet(other):
        pl.semaphore_signal(barrier, inc=1, device_id=other, device_id_type=LOGICAL)

    first_x, last_x = here["x"] == 0, here["x"] == SUB["x"] - 1
    first_block, last_block = my_space == 0, my_space == n_space - 1
    up_step = last_x & (here["zhi"] < FOLLOW)

    def greet_space(other):
        pl.semaphore_signal(barrier, inc=1, device_id={"space": other}, device_id_type=MESH)

    for other in (left, right):
        pl.semaphore_signal(barrier, inc=1, device_id={"inst": other}, device_id_type=MESH)
    pl.when(jnp.logical_not(first_x))(lambda: greet_space(preceding))
    pl.when(jnp.logical_not(last_block))(lambda: greet_space(following))
    sides = jnp.where(first_block | last_x, 1, 2)

    @pl.when(collects)
    def _():
        for offsets in reversed(PLANE):
            greet(on_plane(offsets))
        for offsets in LINE[1:]:
            greet(on_line(0, offsets))
        for zhi in range(1, FOLLOW + 1):
            for offsets in LINE:
                greet(on_line(zhi, offsets))

    def columns(chunk):
        return pl.ds(chunk * WIDTH, WIDTH)

    def to_right(hop, chunk):
        src = mine if hop == 1 else fromleft.at[hop - 2]
        return pltpu.make_async_remote_copy(
            src_ref=src.at[:, columns(chunk)],
            dst_ref=fromleft.at[hop - 1, :, columns(chunk)],
            send_sem=sr_sem.at[hop - 1, chunk],
            recv_sem=rl_sem.at[hop - 1, chunk],
            device_id={"inst": right},
            device_id_type=MESH,
        )

    def to_left(hop, chunk):
        src = mine if hop == 1 else fromright.at[hop - 2]
        return pltpu.make_async_remote_copy(
            src_ref=src.at[:, columns(chunk)],
            dst_ref=fromright.at[hop - 1, :, columns(chunk)],
            send_sem=sl_sem.at[hop - 1, chunk],
            recv_sem=rr_sem.at[hop - 1, chunk],
            device_id={"inst": left},
            device_id_type=MESH,
        )

    def going(hop):
        rights = [c for c in range(CHUNKS) if hop < half or c < CHUNKS // 2]
        lefts = [c for c in reversed(range(CHUNKS)) if hop < half or c >= CHUNKS // 2]
        return list(zip(rights, lefts))

    def block(ref, lanes):
        got = []
        for group in range(DEEP // 16):
            pair = ref[pl.ds(16 * group, 16), lanes].astype(F32)
            got += [pair[0:CX], pair[CX : 2 * CX]]
        return got

    def lane_block(j):
        return pl.ds(pl.multiple_of(j * LANES, LANES), LANES)

    for copy in loads[0:5]:
        copy.wait()

    def pressure(j, carry):
        planes = block(mine, lane_block(j))
        for i in range(HELD):
            total = pw[0] * planes[i * COMP]
            for k in range(1, COMP):
                total = total + pw[k] * planes[i * COMP + k]
            pf[pl.ds(pl.multiple_of(j * CX, CX), CX), pl.ds(i * LANES, LANES)] = total
        return carry

    lax.fori_loop(0, NB_LANE, pressure, 0)

    cell = index[...]
    high = ((cell >> 7) & 7) * CX + (cell >> 10)
    low = cell & (LANES - 1)
    at_high = (lax.broadcasted_iota(jnp.int32, (CX * NB_LANE, ROWS), 0) == high).astype(F32)
    at_low = lax.broadcasted_iota(jnp.int32, (LANES, ROWS), 0) == low
    live = lax.broadcasted_iota(jnp.int32, (1, ROWS), 1) < count[0, 0]
    lag = jnp.where(owner[...] == 0, shift[my_blade * BPG], shift[my_blade * BPG + 1])
    slot = lax.broadcasted_iota(jnp.int32, (ninst, ROWS), 0)
    picks = [(((my_inst * HELD + i - lag) & (ninst - 1)) == slot) & live for i in range(HELD)]

    rows = dot(pf[...], at_high, ((0,), (0,)))
    placed = jnp.zeros((ninst, ROWS), F32)
    for i in range(HELD):
        prow = jnp.sum(jnp.where(at_low, rows[i * LANES : (i + 1) * LANES], 0.0), axis=0, keepdims=True)
        placed = placed + jnp.where(picks[i], prow, 0.0)
    for copy in loads[5:7]:
        copy.wait()
    force = dot(placed, phi[...], ((1,), (1,)))
    first_half = lax.broadcasted_iota(jnp.int32, (CX, LANES), 1) < MODES
    part[0] = jnp.where(first_half, force[0:CX], force[CX : 2 * CX])

    def tile(src, dst, stage, other):
        return pltpu.make_async_remote_copy(
            src_ref=src,
            dst_ref=dst,
            send_sem=as_sem.at[stage],
            recv_sem=ar_sem.at[stage],
            device_id=other,
            device_id_type=LOGICAL,
        )

    def tiles(number, sem):
        some = box1.at[pl.ds(0, number)]
        return pltpu.make_async_copy(some, some, sem)

    def sum_box(first, box, number, stage):
        pltpu.make_async_copy(box, box, ar_sem.at[stage]).wait()
        total = first
        for k in range(number):
            total = total + box[k]
        return total

    @pl.when(collects)
    def _():
        pl.semaphore_wait(barrier, 2 + len(PLANE) + len(LINE) - 1 + sides)
        for k, offsets in enumerate(LINE[1:]):
            tile(part.at[0], box0.at[FOLLOW * len(LINE) + k], 0, on_line(0, offsets)).start()

    @pl.when(jnp.logical_not(collects))
    def _():
        pl.semaphore_wait(barrier, 2 + len(LINE) + sides)
        for k, offsets in enumerate(LINE):
            tile(part.at[0], box0.at[(here["zhi"] - 1) * len(LINE) + k], 0, on_line(0, offsets)).start()

    for c_right, c_left in going(1):
        to_right(1, c_right).start()
        to_left(1, c_left).start()

    hrow[...] = jnp.zeros_like(hrow)
    for group in range(DEEP // 16):
        pair = mine[pl.ds(16 * group, 16), :].astype(F32)
        for odd in range(2):
            plane = 2 * group + odd
            hrow[0, pl.ds(plane, 1), :] = pair[odd * CX : odd * CX + 1]
            hrow[1, pl.ds(plane, 1), :] = pair[odd * CX + CX - 1 : odd * CX + CX]
    for side in range(2):
        hsend[side] = hrow[side].astype(jnp.bfloat16)
    halos = []
    for side, other in ((0, preceding), (1, following)):
        halos.append(
            pltpu.make_async_remote_copy(
                src_ref=hsend.at[side],
                dst_ref=hrecv.at[side],
                send_sem=hs_sem.at[side],
                recv_sem=hr_sem.at[side],
                device_id={"space": other},
                device_id_type=MESH,
            )
        )

    pl.when(jnp.logical_not(first_block))(halos[0].start)
    pl.when(jnp.logical_not(last_block | up_step))(halos[1].start)

    for group in range(DEEP // 16):
        pair = mine[pl.ds(16 * group, 16), :].astype(F32)
        ahead = pltpu.roll(pair, NC - 1, 1)
        behind = pltpu.roll(pair, 1, 1)
        dcs[pl.ds(16 * group, 16), :] = ahead - behind
        out[pl.ds(16 * group, 16), :] = pair - 0.25 * (ahead + behind)

    def receive(hop):
        onward = going(hop + 1) if hop < half else []
        for pair in going(hop):
            to_right(hop, pair[0]).wait_recv()
            if pair[0] in [c for c, _ in onward]:
                to_right(hop + 1, pair[0]).start()
            to_left(hop, pair[1]).wait_recv()
            if pair[1] in [c for _, c in onward]:
                to_left(hop + 1, pair[1]).start()

    receive(1)

    @pl.when(collects)
    def _():
        part[1] = sum_box(part[0], box0, (FOLLOW + 1) * len(LINE) - 1, 0)
        for k, offsets in enumerate(PLANE):
            tile(part.at[1], box1.at[k], 1, on_plane(offsets)).start()

    layer = lax.broadcasted_iota(jnp.int32, (CX, LANES), 0)

    def local(j, carry):
        lanes = lane_block(j)
        planes = block(mine, lanes)
        for i in range(HELD):
            dx, dc = [], []
            for k in range(COMP):
                p = i * COMP + k
                up = jnp.where(layer == CX - 1, hrow[0, pl.ds(p, 1), lanes], pltpu.roll(planes[p], CX - 1, 0))
                down = jnp.where(layer == 0, hrow[1, pl.ds(p, 1), lanes], pltpu.roll(planes[p], 1, 0))
                dx.append(up - down)
                dc.append(dcs[pl.ds(p * CX, CX), lanes])
                at = pl.ds(p * CX, CX)
                value = out[at, lanes] - 0.25 * (up + down)
                for r in range(HELD):
                    value = value + spectral(i - r, ninst) * planes[r * COMP + k]
                out[at, lanes] = value
            for k in range(COMP):
                at = pl.ds((i * COMP + k) * CX, CX)
                flow = fx[k, 0] * dx[0] + fc[k, 0] * dc[0]
                for c in range(1, COMP):
                    flow = flow + fx[k, c] * dx[c] + fc[k, c] * dc[c]
                out[at, lanes] = out[at, lanes] + 0.5 * flow
        return carry

    def add_blocks(sources, first, last):
        def add(j, carry):
            lanes = lane_block(j)
            sums = [out[pl.ds(p * CX, CX), lanes] for p in range(PLANES)]
            for ref, offset in sources:
                planes = block(ref, lanes)
                for i in range(HELD):
                    for k in range(COMP):
                        for r in range(HELD):
                            sums[i * COMP + k] += spectral(HELD * offset + i - r, ninst) * planes[r * COMP + k]
            for p in range(PLANES):
                out[pl.ds(p * CX, CX), lanes] = sums[p]
            return carry

        lax.fori_loop(first, last, add, 0)

    for hop in range(1, half):
        if hop > 1:
            receive(hop)
        add_blocks([(fromleft.at[hop - 1], hop), (fromright.at[hop - 1], -hop)], 0, NB_LANE)

    for copy in loads[7:]:
        copy.wait()
    pl.when(jnp.logical_not(last_block))(halos[0].wait_recv)
    pl.when(up_step)(halos[1].start)
    pl.when(jnp.logical_not(first_block))(halos[1].wait_recv)

    def neighbour(side, end):
        @pl.when(end)
        def _():
            hrow[side] = jnp.zeros((16, NC), F32)

        @pl.when(jnp.logical_not(end))
        def _():
            hrow[side] = hrecv[side].astype(F32)

    neighbour(0, last_block)
    neighbour(1, first_block)
    lax.fori_loop(0, NB_LANE, local, 0)

    @pl.when(collects)
    def _():
        whole[...] = sum_box(part[1], box1, len(PLANE), 1)
        for zhi in range(1, FOLLOW + 1):
            tile(whole, whole, 2, on_line(zhi, LINE[0])).start()

    receive(half)
    add_blocks([(fromleft.at[half - 1], half)], 0, NB_LANE // 2)
    add_blocks([(fromright.at[half - 1], -half)], NB_LANE // 2, NB_LANE)

    @pl.when(jnp.logical_not(collects))
    def _():
        pltpu.make_async_copy(whole, whole, ar_sem.at[2]).wait()

    total = whole[...]
    rigid = jnp.concatenate([stiff[...], stiff[...]], axis=1)
    amp = total / rigid
    both = jnp.concatenate([jnp.where(first_half, amp, 0.0), jnp.where(first_half, 0.0, amp)], axis=0)
    moved = dot(both, phi[...], ((1,), (0,)))
    spread = []
    for i in range(HELD):
        disp = jnp.sum(jnp.where(picks[i], moved, 0.0), axis=0, keepdims=True)
        spread.append(jnp.where(at_low, disp, 0.0))
    hit = dot(at_high, jnp.concatenate(spread, axis=0), ((1,), (1,)))
    for i in range(HELD):
        for j in range(NB_LANE):
            field[pl.ds(i * CX, CX), pl.ds(j * LANES, LANES)] = hit[j * CX : (j + 1) * CX, i * LANES : (i + 1) * LANES]

    for hop in range(1, half + 1):
        for c_right, c_left in going(hop):
            to_right(hop, c_right).wait_send()
            to_left(hop, c_left).wait_send()
    pl.when(jnp.logical_not(first_block))(halos[0].wait_send)
    pl.when(jnp.logical_not(last_block))(halos[1].wait_send)

    @pl.when(collects)
    def _():
        tiles(len(LINE) - 1, as_sem.at[0]).wait()
        tiles(len(PLANE), as_sem.at[1]).wait()
        tiles(FOLLOW, as_sem.at[2]).wait()

    @pl.when(jnp.logical_not(collects))
    def _():
        tiles(len(LINE), as_sem.at[0]).wait()


def body(sizes, state, fx, fc, pw, cpl, modes, stiff, index, count, owner, shift):
    n_space, n_inst, n_blade = sizes
    half = n_inst // 2
    assert sizes == (SUB["zhi"] * SUB["x"], SUB["y"], SUB["zlo"] * SUB["core"])
    vmem = pl.BlockSpec(memory_space=pltpu.VMEM)
    hbm = pl.BlockSpec(memory_space=pltpu.HBM)
    dma = pltpu.SemaphoreType.DMA
    operands = (
        state.reshape(DEEP, NC),
        fx,
        fc,
        pw,
        cpl,
        modes.reshape(MODES, ROWS),
        stiff.reshape(1, MODES),
        index,
        owner,
        shift,
    )
    out, field, gain = pl.pallas_call(
        functools.partial(kernel, sizes),
        out_shape=(jax.ShapeDtypeStruct((DEEP, NC), F32), jax.ShapeDtypeStruct((HELD * CX, NC), F32), jax.ShapeDtypeStruct((COMP,), F32)),
        in_specs=[pl.BlockSpec(memory_space=pltpu.SMEM)] + [hbm] * len(operands),
        out_specs=(vmem, vmem, vmem),
        scratch_shapes=[
            pltpu.VMEM((DEEP, NC), jnp.bfloat16),
            pltpu.VMEM((2 * MODES, ROWS), F32),
            pltpu.SMEM((COMP, COMP), F32),
            pltpu.SMEM((COMP, COMP), F32),
            pltpu.SMEM((COMP,), F32),
            pltpu.VMEM((1, MODES), F32),
            pltpu.VMEM((1, ROWS), jnp.int32),
            pltpu.VMEM((1, ROWS), jnp.int32),
            pltpu.SMEM((n_blade * BPG,), jnp.int32),
            pltpu.VMEM((DEEP, NC), F32),
            pltpu.VMEM((half, DEEP, NC), jnp.bfloat16),
            pltpu.VMEM((half, DEEP, NC), jnp.bfloat16),
            pltpu.VMEM((2, 16, NC), F32),
            pltpu.VMEM((2, 16, NC), jnp.bfloat16),
            pltpu.VMEM((2, 16, NC), jnp.bfloat16),
            pltpu.VMEM((CX * NB_LANE, HELD * LANES), F32),
            pltpu.VMEM((2, CX, LANES), F32),
            pltpu.VMEM(((FOLLOW + 1) * len(LINE) - 1, CX, LANES), F32),
            pltpu.VMEM((len(PLANE), CX, LANES), F32),
            pltpu.VMEM((CX, LANES), F32),
            dma((len(operands) + 1,)),
            dma((half, CHUNKS)),
            dma((half, CHUNKS)),
            dma((half, CHUNKS)),
            dma((half, CHUNKS)),
            dma((2,)),
            dma((2,)),
            dma((3,)),
            dma((3,)),
        ],
        compiler_params=pltpu.CompilerParams(
            collective_id=0, has_side_effects=True, vmem_limit_bytes=24 * 1024 * 1024
        ),
        name="residual",
    )(count, *[pltpu.with_memory_space_constraint(operand, pltpu.HBM) for operand in operands])
    wall = gain[None, :, None, None] * field.reshape(HELD, 1, CX, NC)
    return (out.reshape(HELD, COMP, CX, NC) + wall)[None]


def solution(mesh):
    sizes = (mesh.shape["space"], mesh.shape["inst"], mesh.shape["blade"])
    placed = (
        P("blade", "inst", None, "space", None),
        P(),
        P(),
        P(),
        P(),
        P("blade", None, "space"),
        P(),
        P("blade", "space"),
        P("blade", "space"),
        P("blade", "space"),
        P(),
    )
    return jax.shard_map(
        functools.partial(body, sizes),
        mesh=mesh,
        in_specs=placed,
        out_specs=P("blade", "inst", None, "space", None),
        check_vma=False,
    )
```

```python
import functools
import itertools
import math

import jax
import jax.numpy as jnp
from jax import lax
from jax.experimental import pallas as pl
from jax.experimental.pallas import tpu as pltpu
from jax.sharding import PartitionSpec as P

COMP = 5
CX = 8
NC = 1024
MODES = 64
ROWS = 256
BPG = 2
HELD = 2
PLANES = HELD * COMP
DEEP = PLANES * CX
LANES = 128
NB_LANE = NC // LANES
CHUNKS = 4
WIDTH = NC // CHUNKS
EARLY = 3


HIGH = lax.Precision.HIGHEST
MESH = pl.DeviceIdType.MESH
LOGICAL = pl.DeviceIdType.LOGICAL
F32 = jnp.float32


def spectral(offset, count):
    offset %= count
    if offset == 0:
        return 0.0
    angle = math.pi * offset / count
    return 0.5 * (-1.0) ** offset * math.cos(angle) / math.sin(angle)


def dot(a, b, dims):
    return lax.dot_general(a, b, (dims, ((), ())), precision=HIGH, preferred_element_type=F32)


SUB = {"zhi": 3, "x": 4, "y": 8, "zlo": 4, "core": 2}


STEP = {"core": 1, "zlo": 2, "y": 8, "x": 64, "zhi": 256}


def around(offset, size):
    return min(offset, size - offset)


LINE = list(itertools.product(range(SUB["zlo"]), range(SUB["core"])))
PLANE = sorted(
    (o for o in itertools.product(range(SUB["x"]), range(SUB["y"])) if any(o)),
    key=lambda o: -around(o[0], SUB["x"]) - around(o[1], SUB["y"]),
)
FOLLOW = SUB["zhi"] - 1


def place(space, inst, blade):
    here = {
        "zhi": space // SUB["x"],
        "x": space % SUB["x"],
        "y": inst,
        "zlo": blade // SUB["core"],
        "core": blade % SUB["core"],
    }
    table = {}
    for axis, size in SUB.items():
        table[axis] = []
        for offset in range(size):
            at = here[axis] + offset
            table[axis].append(jnp.where(at >= size, at - size, at) * STEP[axis])
    return here, table


def kernel(
    sizes,
    count,
    state_hbm,
    fx_hbm,
    fc_hbm,
    pw_hbm,
    cpl_hbm,
    modes_hbm,
    stiff_hbm,
    index_hbm,
    owner_hbm,
    shift_hbm,
    out,
    field,
    gain,
    mine,
    phi,
    fx,
    fc,
    pw,
    stiff,
    index,
    owner,
    shift,
    dcs,
    fromleft,
    fromright,
    hrow,
    hsend,
    hrecv,
    pf,
    part,
    box0,
    box1,
    whole,
    load_sem,
    sl_sem,
    rl_sem,
    sr_sem,
    rr_sem,
    hs_sem,
    hr_sem,
    as_sem,
    ar_sem,
):
    n_space, n_inst, n_blade = sizes
    half = n_inst // 2
    ninst = n_inst * HELD
    my_space = lax.axis_index("space")
    my_inst = lax.axis_index("inst")
    my_blade = lax.axis_index("blade")

    moves = (
        (state_hbm, mine),
        (index_hbm, index),
        (pw_hbm, pw),
        (owner_hbm, owner),
        (shift_hbm, shift),
        (modes_hbm, phi.at[pl.ds(0, MODES)]),
        (modes_hbm, phi.at[pl.ds(MODES, MODES)]),
        (fx_hbm, fx),
        (fc_hbm, fc),
        (stiff_hbm, stiff),
        (cpl_hbm, gain),
    )
    loads = [pltpu.make_async_copy(src, dst, load_sem.at[n]) for n, (src, dst) in enumerate(moves)]
    for copy in loads:
        copy.start()

    here, table = place(my_space, my_inst, my_blade)
    column = table["x"][0] + table["y"][0]
    stack = table["zlo"][0] + table["core"][0]
    collects = here["zhi"] == 0

    def on_line(zhi, offsets):
        return column + zhi * STEP["zhi"] + table["zlo"][offsets[0]] + table["core"][offsets[1]]

    def on_plane(offsets):
        return stack + table["x"][offsets[0]] + table["y"][offsets[1]]

    right = lax.rem(my_inst + 1, n_inst)
    left = lax.rem(my_inst + n_inst - 1, n_inst)
    following = lax.rem(my_space + 1, n_space)
    preceding = lax.rem(my_space + n_space - 1, n_space)

    barrier = pltpu.get_barrier_semaphore()

    def greet(other):
        pl.semaphore_signal(barrier, inc=1, device_id=other, device_id_type=LOGICAL)

    first_x, last_x = here["x"] == 0, here["x"] == SUB["x"] - 1
    first_block, last_block = my_space == 0, my_space == n_space - 1
    up_step = last_x & (here["zhi"] < FOLLOW)

    def greet_space(other):
        pl.semaphore_signal(barrier, inc=1, device_id={"space": other}, device_id_type=MESH)

    for other in (left, right):
        pl.semaphore_signal(barrier, inc=1, device_id={"inst": other}, device_id_type=MESH)
    pl.when(jnp.logical_not(first_x))(lambda: greet_space(preceding))
    pl.when(jnp.logical_not(last_block))(lambda: greet_space(following))
    sides = jnp.where(first_block | last_x, 1, 2)

    @pl.when(collects)
    def _():
        for offsets in reversed(PLANE):
            greet(on_plane(offsets))
        for offsets in LINE[1:]:
            greet(on_line(0, offsets))
        for zhi in range(1, FOLLOW + 1):
            for offsets in LINE:
                greet(on_line(zhi, offsets))

    def columns(chunk):
        return pl.ds(chunk * WIDTH, WIDTH)

    def to_right(hop, chunk):
        src = mine if hop == 1 else fromleft.at[hop - 2]
        return pltpu.make_async_remote_copy(
            src_ref=src.at[:, columns(chunk)],
            dst_ref=fromleft.at[hop - 1, :, columns(chunk)],
            send_sem=sr_sem.at[hop - 1, chunk],
            recv_sem=rl_sem.at[hop - 1, chunk],
            device_id={"inst": right},
            device_id_type=MESH,
        )

    def to_left(hop, chunk):
        src = mine if hop == 1 else fromright.at[hop - 2]
        return pltpu.make_async_remote_copy(
            src_ref=src.at[:, columns(chunk)],
            dst_ref=fromright.at[hop - 1, :, columns(chunk)],
            send_sem=sl_sem.at[hop - 1, chunk],
            recv_sem=rr_sem.at[hop - 1, chunk],
            device_id={"inst": left},
            device_id_type=MESH,
        )

    def going(hop):
        rights = [c for c in range(CHUNKS) if hop < half or c < CHUNKS // 2]
        lefts = [c for c in reversed(range(CHUNKS)) if hop < half or c >= CHUNKS // 2]
        return list(zip(rights, lefts))

    def block(ref, lanes):
        got = []
        for group in range(DEEP // 16):
            pair = ref[pl.ds(16 * group, 16), lanes].astype(F32)
            got += [pair[0:CX], pair[CX : 2 * CX]]
        return got

    def lane_block(j):
        return pl.ds(pl.multiple_of(j * LANES, LANES), LANES)

    for copy in loads[0:5]:
        copy.wait()

    def pressure(j, carry):
        planes = block(mine, lane_block(j))
        for i in range(HELD):
            total = pw[0] * planes[i * COMP]
            for k in range(1, COMP):
                total = total + pw[k] * planes[i * COMP + k]
            pf[pl.ds(pl.multiple_of(j * CX, CX), CX), pl.ds(i * LANES, LANES)] = total
        return carry

    lax.fori_loop(0, NB_LANE, pressure, 0)

    cell = index[...]
    high = ((cell >> 7) & 7) * CX + (cell >> 10)
    low = cell & (LANES - 1)
    at_high = (lax.broadcasted_iota(jnp.int32, (CX * NB_LANE, ROWS), 0) == high).astype(F32)
    at_low = lax.broadcasted_iota(jnp.int32, (LANES, ROWS), 0) == low
    live = lax.broadcasted_iota(jnp.int32, (1, ROWS), 1) < count[0, 0]
    lag = jnp.where(owner[...] == 0, shift[my_blade * BPG], shift[my_blade * BPG + 1])
    slot = lax.broadcasted_iota(jnp.int32, (ninst, ROWS), 0)
    picks = [(((my_inst * HELD + i - lag) & (ninst - 1)) == slot) & live for i in range(HELD)]

    rows = dot(pf[...], at_high, ((0,), (0,)))
    placed = jnp.zeros((ninst, ROWS), F32)
    for i in range(HELD):
        prow = jnp.sum(jnp.where(at_low, rows[i * LANES : (i + 1) * LANES], 0.0), axis=0, keepdims=True)
        placed = placed + jnp.where(picks[i], prow, 0.0)
    for copy in loads[5:7]:
        copy.wait()
    force = dot(placed, phi[...], ((1,), (1,)))
    first_half = lax.broadcasted_iota(jnp.int32, (CX, LANES), 1) < MODES
    part[0] = jnp.where(first_half, force[0:CX], force[CX : 2 * CX])

    def tile(src, dst, stage, other):
        return pltpu.make_async_remote_copy(
            src_ref=src,
            dst_ref=dst,
            send_sem=as_sem.at[stage],
            recv_sem=ar_sem.at[stage],
            device_id=other,
            device_id_type=LOGICAL,
        )

    def tiles(number, sem):
        some = box1.at[pl.ds(0, number)]
        return pltpu.make_async_copy(some, some, sem)

    def sum_box(first, box, number, stage):
        pltpu.make_async_copy(box, box, ar_sem.at[stage]).wait()
        total = first
        for k in range(number):
            total = total + box[k]
        return total

    @pl.when(collects)
    def _():
        pl.semaphore_wait(barrier, 2 + len(PLANE) + len(LINE) - 1 + sides)
        for k, offsets in enumerate(LINE[1:]):
            tile(part.at[0], box0.at[FOLLOW * len(LINE) + k], 0, on_line(0, offsets)).start()

    @pl.when(jnp.logical_not(collects))
    def _():
        pl.semaphore_wait(barrier, 2 + len(LINE) + sides)
        for k, offsets in enumerate(LINE):
            tile(part.at[0], box0.at[(here["zhi"] - 1) * len(LINE) + k], 0, on_line(0, offsets)).start()

    for c_right, c_left in going(1):
        to_right(1, c_right).start()
        to_left(1, c_left).start()

    hrow[...] = jnp.zeros_like(hrow)
    for group in range(DEEP // 16):
        pair = mine[pl.ds(16 * group, 16), :].astype(F32)
        for odd in range(2):
            plane = 2 * group + odd
            hrow[0, pl.ds(plane, 1), :] = pair[odd * CX : odd * CX + 1]
            hrow[1, pl.ds(plane, 1), :] = pair[odd * CX + CX - 1 : odd * CX + CX]
    for side in range(2):
        hsend[side] = hrow[side].astype(jnp.bfloat16)
    halos = []
    for side, other in ((0, preceding), (1, following)):
        halos.append(
            pltpu.make_async_remote_copy(
                src_ref=hsend.at[side],
                dst_ref=hrecv.at[side],
                send_sem=hs_sem.at[side],
                recv_sem=hr_sem.at[side],
                device_id={"space": other},
                device_id_type=MESH,
            )
        )

    pl.when(jnp.logical_not(first_block))(halos[0].start)
    pl.when(jnp.logical_not(last_block | up_step))(halos[1].start)

    for group in range(DEEP // 16):
        pair = mine[pl.ds(16 * group, 16), :].astype(F32)
        ahead = pltpu.roll(pair, NC - 1, 1)
        behind = pltpu.roll(pair, 1, 1)
        dcs[pl.ds(16 * group, 16), :] = ahead - behind
        out[pl.ds(16 * group, 16), :] = pair - 0.25 * (ahead + behind)

    def receive(hop, first=0, last=None):
        onward = going(hop + 1) if hop < half else []
        for pair in going(hop)[first:last]:
            to_right(hop, pair[0]).wait_recv()
            if pair[0] in [c for c, _ in onward]:
                to_right(hop + 1, pair[0]).start()
            to_left(hop, pair[1]).wait_recv()
            if pair[1] in [c for _, c in onward]:
                to_left(hop + 1, pair[1]).start()

    receive(1)

    @pl.when(up_step)
    def _():
        halos[0].wait_recv()
        halos[1].start()

    receive(2, 0, EARLY)

    @pl.when(collects)
    def _():
        part[1] = sum_box(part[0], box0, (FOLLOW + 1) * len(LINE) - 1, 0)
        for k, offsets in enumerate(PLANE):
            tile(part.at[1], box1.at[k], 1, on_plane(offsets)).start()

    layer = lax.broadcasted_iota(jnp.int32, (CX, LANES), 0)

    def local(j, carry):
        lanes = lane_block(j)
        planes = block(mine, lanes)
        for i in range(HELD):
            dx, dc = [], []
            for k in range(COMP):
                p = i * COMP + k
                up = jnp.where(layer == CX - 1, hrow[0, pl.ds(p, 1), lanes], pltpu.roll(planes[p], CX - 1, 0))
                down = jnp.where(layer == 0, hrow[1, pl.ds(p, 1), lanes], pltpu.roll(planes[p], 1, 0))
                dx.append(up - down)
                dc.append(dcs[pl.ds(p * CX, CX), lanes])
                at = pl.ds(p * CX, CX)
                value = out[at, lanes] - 0.25 * (up + down)
                for r in range(HELD):
                    value = value + spectral(i - r, ninst) * planes[r * COMP + k]
                out[at, lanes] = value
            for k in range(COMP):
                at = pl.ds((i * COMP + k) * CX, CX)
                flow = fx[k, 0] * dx[0] + fc[k, 0] * dc[0]
                for c in range(1, COMP):
                    flow = flow + fx[k, c] * dx[c] + fc[k, c] * dc[c]
                out[at, lanes] = out[at, lanes] + 0.5 * flow
        return carry

    def add_blocks(sources, first, last):
        def add(j, carry):
            lanes = lane_block(j)
            sums = [out[pl.ds(p * CX, CX), lanes] for p in range(PLANES)]
            for ref, offset in sources:
                planes = block(ref, lanes)
                for i in range(HELD):
                    for k in range(COMP):
                        for r in range(HELD):
                            sums[i * COMP + k] += spectral(HELD * offset + i - r, ninst) * planes[r * COMP + k]
            for p in range(PLANES):
                out[pl.ds(p * CX, CX), lanes] = sums[p]
            return carry

        lax.fori_loop(first, last, add, 0)

    for hop in range(1, half):
        if hop > 1:
            receive(hop, EARLY if hop == 2 else 0)
        add_blocks([(fromleft.at[hop - 1], hop), (fromright.at[hop - 1], -hop)], 0, NB_LANE)

    for copy in loads[7:]:
        copy.wait()
    pl.when(jnp.logical_not(last_block | up_step))(halos[0].wait_recv)
    pl.when(jnp.logical_not(first_block))(halos[1].wait_recv)

    def neighbour(side, end):
        @pl.when(end)
        def _():
            hrow[side] = jnp.zeros((16, NC), F32)

        @pl.when(jnp.logical_not(end))
        def _():
            hrow[side] = hrecv[side].astype(F32)

    neighbour(0, last_block)
    neighbour(1, first_block)
    lax.fori_loop(0, NB_LANE, local, 0)

    receive(half)
    add_blocks([(fromleft.at[half - 1], half)], 0, NB_LANE // 2)
    add_blocks([(fromright.at[half - 1], -half)], NB_LANE // 2, NB_LANE)

    @pl.when(collects)
    def _():
        whole[...] = sum_box(part[1], box1, len(PLANE), 1)
        for zhi in range(1, FOLLOW + 1):
            tile(whole, whole, 2, on_line(zhi, LINE[0])).start()

    @pl.when(jnp.logical_not(collects))
    def _():
        pltpu.make_async_copy(whole, whole, ar_sem.at[2]).wait()

    total = whole[...]
    rigid = jnp.concatenate([stiff[...], stiff[...]], axis=1)
    amp = total / rigid
    both = jnp.concatenate([jnp.where(first_half, amp, 0.0), jnp.where(first_half, 0.0, amp)], axis=0)
    moved = dot(both, phi[...], ((1,), (0,)))
    spread = []
    for i in range(HELD):
        disp = jnp.sum(jnp.where(picks[i], moved, 0.0), axis=0, keepdims=True)
        spread.append(jnp.where(at_low, disp, 0.0))
    hit = dot(at_high, jnp.concatenate(spread, axis=0), ((1,), (1,)))
    for i in range(HELD):
        for j in range(NB_LANE):
            field[pl.ds(i * CX, CX), pl.ds(j * LANES, LANES)] = hit[j * CX : (j + 1) * CX, i * LANES : (i + 1) * LANES]

    for hop in range(1, half + 1):
        for c_right, c_left in going(hop):
            to_right(hop, c_right).wait_send()
            to_left(hop, c_left).wait_send()
    pl.when(jnp.logical_not(first_block))(halos[0].wait_send)
    pl.when(jnp.logical_not(last_block))(halos[1].wait_send)

    @pl.when(collects)
    def _():
        tiles(len(LINE) - 1, as_sem.at[0]).wait()
        tiles(len(PLANE), as_sem.at[1]).wait()
        tiles(FOLLOW, as_sem.at[2]).wait()

    @pl.when(jnp.logical_not(collects))
    def _():
        tiles(len(LINE), as_sem.at[0]).wait()


def body(sizes, state, fx, fc, pw, cpl, modes, stiff, index, count, owner, shift):
    n_space, n_inst, n_blade = sizes
    half = n_inst // 2
    assert sizes == (SUB["zhi"] * SUB["x"], SUB["y"], SUB["zlo"] * SUB["core"])
    vmem = pl.BlockSpec(memory_space=pltpu.VMEM)
    hbm = pl.BlockSpec(memory_space=pltpu.HBM)
    dma = pltpu.SemaphoreType.DMA
    operands = (
        state.reshape(DEEP, NC),
        fx,
        fc,
        pw,
        cpl,
        modes.reshape(MODES, ROWS),
        stiff.reshape(1, MODES),
        index,
        owner,
        shift,
    )
    out, field, gain = pl.pallas_call(
        functools.partial(kernel, sizes),
        out_shape=(jax.ShapeDtypeStruct((DEEP, NC), F32), jax.ShapeDtypeStruct((HELD * CX, NC), F32), jax.ShapeDtypeStruct((COMP,), F32)),
        in_specs=[pl.BlockSpec(memory_space=pltpu.SMEM)] + [hbm] * len(operands),
        out_specs=(vmem, vmem, vmem),
        scratch_shapes=[
            pltpu.VMEM((DEEP, NC), jnp.bfloat16),
            pltpu.VMEM((2 * MODES, ROWS), F32),
            pltpu.SMEM((COMP, COMP), F32),
            pltpu.SMEM((COMP, COMP), F32),
            pltpu.SMEM((COMP,), F32),
            pltpu.VMEM((1, MODES), F32),
            pltpu.VMEM((1, ROWS), jnp.int32),
            pltpu.VMEM((1, ROWS), jnp.int32),
            pltpu.SMEM((n_blade * BPG,), jnp.int32),
            pltpu.VMEM((DEEP, NC), F32),
            pltpu.VMEM((half, DEEP, NC), jnp.bfloat16),
            pltpu.VMEM((half, DEEP, NC), jnp.bfloat16),
            pltpu.VMEM((2, 16, NC), F32),
            pltpu.VMEM((2, 16, NC), jnp.bfloat16),
            pltpu.VMEM((2, 16, NC), jnp.bfloat16),
            pltpu.VMEM((CX * NB_LANE, HELD * LANES), F32),
            pltpu.VMEM((2, CX, LANES), F32),
            pltpu.VMEM(((FOLLOW + 1) * len(LINE) - 1, CX, LANES), F32),
            pltpu.VMEM((len(PLANE), CX, LANES), F32),
            pltpu.VMEM((CX, LANES), F32),
            dma((len(operands) + 1,)),
            dma((half, CHUNKS)),
            dma((half, CHUNKS)),
            dma((half, CHUNKS)),
            dma((half, CHUNKS)),
            dma((2,)),
            dma((2,)),
            dma((3,)),
            dma((3,)),
        ],
        compiler_params=pltpu.CompilerParams(
            collective_id=0, has_side_effects=True, vmem_limit_bytes=24 * 1024 * 1024
        ),
        name="residual",
    )(count, *[pltpu.with_memory_space_constraint(operand, pltpu.HBM) for operand in operands])
    wall = gain[None, :, None, None] * field.reshape(HELD, 1, CX, NC)
    return (out.reshape(HELD, COMP, CX, NC) + wall)[None]


def solution(mesh):
    sizes = (mesh.shape["space"], mesh.shape["inst"], mesh.shape["blade"])
    placed = (
        P("blade", "inst", None, "space", None),
        P(),
        P(),
        P(),
        P(),
        P("blade", None, "space"),
        P(),
        P("blade", "space"),
        P("blade", "space"),
        P("blade", "space"),
        P(),
    )
    return jax.shard_map(
        functools.partial(body, sizes),
        mesh=mesh,
        in_specs=placed,
        out_specs=P("blade", "inst", None, "space", None),
        check_vma=False,
    )
```

```python
import functools
import itertools
import math

import jax
import jax.numpy as jnp
from jax import lax
from jax.experimental import pallas as pl
from jax.experimental.pallas import tpu as pltpu
from jax.sharding import PartitionSpec as P

COMP = 5
CX = 8
NC = 1024
MODES = 64
ROWS = 256
BPG = 2
HELD = 2
PLANES = HELD * COMP
DEEP = PLANES * CX
LANES = 128
NB_LANE = NC // LANES
CHUNKS = 4
WIDTH = NC // CHUNKS
EARLY = 3


HIGH = lax.Precision.HIGHEST
MESH = pl.DeviceIdType.MESH
LOGICAL = pl.DeviceIdType.LOGICAL
F32 = jnp.float32


def spectral(offset, count):
    offset %= count
    if offset == 0:
        return 0.0
    angle = math.pi * offset / count
    return 0.5 * (-1.0) ** offset * math.cos(angle) / math.sin(angle)


def dot(a, b, dims):
    return lax.dot_general(a, b, (dims, ((), ())), precision=HIGH, preferred_element_type=F32)


SUB = {"zhi": 3, "x": 4, "y": 8, "zlo": 4, "core": 2}


STEP = {"core": 1, "zlo": 2, "y": 8, "x": 64, "zhi": 256}


def around(offset, size):
    return min(offset, size - offset)


LINE = list(itertools.product(range(SUB["zlo"]), range(SUB["core"])))
PLANE = sorted(
    (o for o in itertools.product(range(SUB["x"]), range(SUB["y"])) if any(o)),
    key=lambda o: -around(o[0], SUB["x"]) - around(o[1], SUB["y"]),
)
FOLLOW = SUB["zhi"] - 1


def place(space, inst, blade):
    here = {
        "zhi": space // SUB["x"],
        "x": space % SUB["x"],
        "y": inst,
        "zlo": blade // SUB["core"],
        "core": blade % SUB["core"],
    }
    table = {}
    for axis, size in SUB.items():
        table[axis] = []
        for offset in range(size):
            at = here[axis] + offset
            table[axis].append(jnp.where(at >= size, at - size, at) * STEP[axis])
    return here, table


def parts(values):
    upper = values.astype(jnp.bfloat16)
    return upper, (values - upper.astype(F32)).astype(jnp.bfloat16)


def kernel(
    sizes,
    count,
    state_hbm,
    fx_hbm,
    fc_hbm,
    pw_hbm,
    cpl_hbm,
    modes_hbm,
    stiff_hbm,
    index_hbm,
    owner_hbm,
    shift_hbm,
    out,
    field,
    gain,
    mine,
    phi,
    fx,
    fc,
    pw,
    stiff,
    index,
    owner,
    shift,
    phis,
    low_rows,
    dcs,
    fromleft,
    fromright,
    hrow,
    hsend,
    hrecv,
    pf,
    part,
    box0,
    box1,
    whole,
    load_sem,
    sl_sem,
    rl_sem,
    sr_sem,
    rr_sem,
    hs_sem,
    hr_sem,
    as_sem,
    ar_sem,
):
    n_space, n_inst, n_blade = sizes
    half = n_inst // 2
    ninst = n_inst * HELD
    my_space = lax.axis_index("space")
    my_inst = lax.axis_index("inst")
    my_blade = lax.axis_index("blade")

    moves = (
        (state_hbm, mine),
        (index_hbm, index),
        (pw_hbm, pw),
        (owner_hbm, owner),
        (shift_hbm, shift),
        (modes_hbm, phi.at[pl.ds(0, MODES)]),
        (modes_hbm, phi.at[pl.ds(MODES, MODES)]),
        (fx_hbm, fx),
        (fc_hbm, fc),
        (stiff_hbm, stiff),
        (cpl_hbm, gain),
    )
    loads = [pltpu.make_async_copy(src, dst, load_sem.at[n]) for n, (src, dst) in enumerate(moves)]
    for copy in loads:
        copy.start()

    here, table = place(my_space, my_inst, my_blade)
    column = table["x"][0] + table["y"][0]
    stack = table["zlo"][0] + table["core"][0]
    collects = here["zhi"] == 0

    def on_line(zhi, offsets):
        return column + zhi * STEP["zhi"] + table["zlo"][offsets[0]] + table["core"][offsets[1]]

    def on_plane(offsets):
        return stack + table["x"][offsets[0]] + table["y"][offsets[1]]

    right = lax.rem(my_inst + 1, n_inst)
    left = lax.rem(my_inst + n_inst - 1, n_inst)
    following = lax.rem(my_space + 1, n_space)
    preceding = lax.rem(my_space + n_space - 1, n_space)

    barrier = pltpu.get_barrier_semaphore()

    def greet(other):
        pl.semaphore_signal(barrier, inc=1, device_id=other, device_id_type=LOGICAL)

    first_x, last_x = here["x"] == 0, here["x"] == SUB["x"] - 1
    first_block, last_block = my_space == 0, my_space == n_space - 1
    up_step = last_x & (here["zhi"] < FOLLOW)

    def greet_space(other):
        pl.semaphore_signal(barrier, inc=1, device_id={"space": other}, device_id_type=MESH)

    for other in (left, right):
        pl.semaphore_signal(barrier, inc=1, device_id={"inst": other}, device_id_type=MESH)
    pl.when(jnp.logical_not(first_x))(lambda: greet_space(preceding))
    pl.when(jnp.logical_not(last_block))(lambda: greet_space(following))
    sides = jnp.where(first_block | last_x, 1, 2)

    @pl.when(collects)
    def _():
        for offsets in PLANE:
            greet(on_plane(offsets))
        for offsets in LINE[1:]:
            greet(on_line(0, offsets))
        for zhi in range(1, FOLLOW + 1):
            for offsets in LINE:
                greet(on_line(zhi, offsets))

    def columns(chunk):
        return pl.ds(chunk * WIDTH, WIDTH)

    def to_right(hop, chunk):
        src = mine if hop == 1 else fromleft.at[hop - 2]
        return pltpu.make_async_remote_copy(
            src_ref=src.at[:, columns(chunk)],
            dst_ref=fromleft.at[hop - 1, :, columns(chunk)],
            send_sem=sr_sem.at[hop - 1, chunk],
            recv_sem=rl_sem.at[hop - 1, chunk],
            device_id={"inst": right},
            device_id_type=MESH,
        )

    def to_left(hop, chunk):
        src = mine if hop == 1 else fromright.at[hop - 2]
        return pltpu.make_async_remote_copy(
            src_ref=src.at[:, columns(chunk)],
            dst_ref=fromright.at[hop - 1, :, columns(chunk)],
            send_sem=sl_sem.at[hop - 1, chunk],
            recv_sem=rr_sem.at[hop - 1, chunk],
            device_id={"inst": left},
            device_id_type=MESH,
        )

    def going(hop):
        rights = [c for c in range(CHUNKS) if hop < half or c < CHUNKS // 2]
        lefts = [c for c in reversed(range(CHUNKS)) if hop < half or c >= CHUNKS // 2]
        return list(zip(rights, lefts))

    def block(ref, lanes):
        got = []
        for group in range(DEEP // 16):
            pair = ref[pl.ds(16 * group, 16), lanes].astype(F32)
            got += [pair[0:CX], pair[CX : 2 * CX]]
        return got

    def lane_block(j):
        return pl.ds(pl.multiple_of(j * LANES, LANES), LANES)

    for copy in loads[0:5]:
        copy.wait()

    def pressure(j, carry):
        planes = block(mine, lane_block(j))
        for i in range(HELD):
            total = pw[0] * planes[i * COMP]
            for k in range(1, COMP):
                total = total + pw[k] * planes[i * COMP + k]
            pf[pl.ds(pl.multiple_of(j * CX, CX), CX), pl.ds(i * LANES, LANES)] = total
        return carry

    lax.fori_loop(0, NB_LANE, pressure, 0)

    cell = index[...]
    high = ((cell >> 7) & 7) * CX + (cell >> 10)
    low = cell & (LANES - 1)
    at_high = (lax.broadcasted_iota(jnp.int32, (CX * NB_LANE, ROWS), 0) == high).astype(F32)
    at_low = lax.broadcasted_iota(jnp.int32, (LANES, ROWS), 0) == low
    live = lax.broadcasted_iota(jnp.int32, (1, ROWS), 1) < count[0, 0]
    lag = jnp.where(owner[...] == 0, shift[my_blade * BPG], shift[my_blade * BPG + 1])
    slot = lax.broadcasted_iota(jnp.int32, (ninst, ROWS), 0)
    picks = [(((my_inst * HELD + i - lag) & (ninst - 1)) == slot) & live for i in range(HELD)]

    rows = dot(pf[...], at_high, ((0,), (0,)))
    placed = jnp.zeros((ninst, ROWS), F32)
    for i in range(HELD):
        prow = jnp.sum(jnp.where(at_low, rows[i * LANES : (i + 1) * LANES], 0.0), axis=0, keepdims=True)
        placed = placed + jnp.where(picks[i], prow, 0.0)
    for copy in loads[5:7]:
        copy.wait()
    force = dot(placed, phi[...], ((1,), (1,)))
    first_half = lax.broadcasted_iota(jnp.int32, (CX, LANES), 1) < MODES
    part[0] = jnp.where(first_half, force[0:CX], force[CX : 2 * CX])

    def tile(src, dst, stage, other):
        return pltpu.make_async_remote_copy(
            src_ref=src,
            dst_ref=dst,
            send_sem=as_sem.at[stage],
            recv_sem=ar_sem.at[stage],
            device_id=other,
            device_id_type=LOGICAL,
        )

    def tiles(number, sem):
        some = box1.at[pl.ds(0, number)]
        return pltpu.make_async_copy(some, some, sem)

    def sum_box(first, box, number, stage):
        pltpu.make_async_copy(box, box, ar_sem.at[stage]).wait()
        total = first
        for k in range(number):
            total = total + box[k]
        return total

    @pl.when(collects)
    def _():
        pl.semaphore_wait(barrier, 2 + len(PLANE) + len(LINE) - 1 + sides)
        for k, offsets in enumerate(LINE[1:]):
            tile(part.at[0], box0.at[FOLLOW * len(LINE) + k], 0, on_line(0, offsets)).start()

    @pl.when(jnp.logical_not(collects))
    def _():
        pl.semaphore_wait(barrier, 2 + len(LINE) + sides)
        for k, offsets in enumerate(LINE):
            tile(part.at[0], box0.at[(here["zhi"] - 1) * len(LINE) + k], 0, on_line(0, offsets)).start()

    for c_right, c_left in going(1):
        to_right(1, c_right).start()
        to_left(1, c_left).start()

    hrow[...] = jnp.zeros_like(hrow)
    for group in range(DEEP // 16):
        pair = mine[pl.ds(16 * group, 16), :].astype(F32)
        for odd in range(2):
            plane = 2 * group + odd
            hrow[0, pl.ds(plane, 1), :] = pair[odd * CX : odd * CX + 1]
            hrow[1, pl.ds(plane, 1), :] = pair[odd * CX + CX - 1 : odd * CX + CX]
    for side in range(2):
        hsend[side] = hrow[side].astype(jnp.bfloat16)
    halos = []
    for side, other in ((0, preceding), (1, following)):
        halos.append(
            pltpu.make_async_remote_copy(
                src_ref=hsend.at[side],
                dst_ref=hrecv.at[side],
                send_sem=hs_sem.at[side],
                recv_sem=hr_sem.at[side],
                device_id={"space": other},
                device_id_type=MESH,
            )
        )

    pl.when(jnp.logical_not(first_block))(halos[0].start)
    pl.when(jnp.logical_not(last_block | up_step))(halos[1].start)

    upper, lower = parts(phi[...])
    for n, term in enumerate((upper, upper, lower)):
        phis[pl.ds(2 * MODES * n, 2 * MODES), :] = term
    low_rows[...] = jnp.where(at_low, 1.0, 0.0).T.astype(jnp.bfloat16)

    for group in range(DEEP // 16):
        pair = mine[pl.ds(16 * group, 16), :].astype(F32)
        ahead = pltpu.roll(pair, NC - 1, 1)
        behind = pltpu.roll(pair, 1, 1)
        dcs[pl.ds(16 * group, 16), :] = ahead - behind
        out[pl.ds(16 * group, 16), :] = pair - 0.25 * (ahead + behind)

    def receive(hop, first=0, last=None):
        onward = going(hop + 1) if hop < half else []
        for pair in going(hop)[first:last]:
            to_right(hop, pair[0]).wait_recv()
            if pair[0] in [c for c, _ in onward]:
                to_right(hop + 1, pair[0]).start()
            to_left(hop, pair[1]).wait_recv()
            if pair[1] in [c for _, c in onward]:
                to_left(hop + 1, pair[1]).start()

    receive(1)

    @pl.when(up_step)
    def _():
        halos[0].wait_recv()
        halos[1].start()

    receive(2, 0, EARLY)

    @pl.when(collects)
    def _():
        part[1] = sum_box(part[0], box0, (FOLLOW + 1) * len(LINE) - 1, 0)
        for k, offsets in enumerate(PLANE):
            tile(part.at[1], box1.at[k], 1, on_plane(offsets)).start()

    layer = lax.broadcasted_iota(jnp.int32, (CX, LANES), 0)

    def local(j, carry):
        lanes = lane_block(j)
        planes = block(mine, lanes)
        for i in range(HELD):
            dx, dc = [], []
            for k in range(COMP):
                p = i * COMP + k
                up = jnp.where(layer == CX - 1, hrow[0, pl.ds(p, 1), lanes], pltpu.roll(planes[p], CX - 1, 0))
                down = jnp.where(layer == 0, hrow[1, pl.ds(p, 1), lanes], pltpu.roll(planes[p], 1, 0))
                dx.append(up - down)
                dc.append(dcs[pl.ds(p * CX, CX), lanes])
                at = pl.ds(p * CX, CX)
                value = out[at, lanes] - 0.25 * (up + down)
                for r in range(HELD):
                    value = value + spectral(i - r, ninst) * planes[r * COMP + k]
                out[at, lanes] = value
            for k in range(COMP):
                at = pl.ds((i * COMP + k) * CX, CX)
                flow = fx[k, 0] * dx[0] + fc[k, 0] * dc[0]
                for c in range(1, COMP):
                    flow = flow + fx[k, c] * dx[c] + fc[k, c] * dc[c]
                out[at, lanes] = out[at, lanes] + 0.5 * flow
        return carry

    def add_blocks(sources, first, last):
        def add(j, carry):
            lanes = lane_block(j)
            sums = [out[pl.ds(p * CX, CX), lanes] for p in range(PLANES)]
            for ref, offset in sources:
                planes = block(ref, lanes)
                for i in range(HELD):
                    for k in range(COMP):
                        for r in range(HELD):
                            sums[i * COMP + k] += spectral(HELD * offset + i - r, ninst) * planes[r * COMP + k]
            for p in range(PLANES):
                out[pl.ds(p * CX, CX), lanes] = sums[p]
            return carry

        lax.fori_loop(first, last, add, 0)

    for hop in range(1, half):
        if hop > 1:
            receive(hop, EARLY if hop == 2 else 0)
        add_blocks([(fromleft.at[hop - 1], hop), (fromright.at[hop - 1], -hop)], 0, NB_LANE)

    for copy in loads[7:]:
        copy.wait()
    pl.when(jnp.logical_not(last_block | up_step))(halos[0].wait_recv)
    pl.when(jnp.logical_not(first_block))(halos[1].wait_recv)

    def neighbour(side, end):
        @pl.when(end)
        def _():
            hrow[side] = jnp.zeros((16, NC), F32)

        @pl.when(jnp.logical_not(end))
        def _():
            hrow[side] = hrecv[side].astype(F32)

    neighbour(0, last_block)
    neighbour(1, first_block)
    lax.fori_loop(0, NB_LANE, local, 0)

    @pl.when(collects)
    def _():
        whole[...] = sum_box(part[1], box1, len(PLANE), 1)
        for zhi in range(1, FOLLOW + 1):
            tile(whole, whole, 2, on_line(zhi, LINE[0])).start()

    receive(half)
    add_blocks([(fromleft.at[half - 1], half)], 0, NB_LANE // 2)
    add_blocks([(fromright.at[half - 1], -half)], NB_LANE // 2, NB_LANE)

    @pl.when(jnp.logical_not(collects))
    def _():
        pltpu.make_async_copy(whole, whole, ar_sem.at[2]).wait()

    total = whole[...]
    rigid = jnp.concatenate([stiff[...], stiff[...]], axis=1)
    amp = total / rigid
    both = jnp.concatenate([jnp.where(first_half, amp, 0.0), jnp.where(first_half, 0.0, amp)], axis=0)
    upper, lower = parts(both)
    moved = jnp.dot(jnp.concatenate([upper, lower, upper], axis=1), phis[...], preferred_element_type=F32)
    spread = []
    for i in range(HELD):
        disp = jnp.sum(jnp.where(picks[i], moved, 0.0), axis=0, keepdims=True)
        spread.append(at_high * disp)
    upper, lower = parts(jnp.concatenate(spread, axis=0))
    hits = [jnp.dot(term, low_rows[...], preferred_element_type=F32) for term in (upper, lower)]
    hit = hits[0] + hits[1]
    for i in range(HELD):
        for j in range(NB_LANE):
            at = (i * NB_LANE + j) * CX
            field[pl.ds(i * CX, CX), pl.ds(j * LANES, LANES)] = hit[at : at + CX]

    for hop in range(1, half + 1):
        for c_right, c_left in going(hop):
            to_right(hop, c_right).wait_send()
            to_left(hop, c_left).wait_send()
    pl.when(jnp.logical_not(first_block))(halos[0].wait_send)
    pl.when(jnp.logical_not(last_block))(halos[1].wait_send)

    @pl.when(collects)
    def _():
        tiles(len(LINE) - 1, as_sem.at[0]).wait()
        tiles(len(PLANE), as_sem.at[1]).wait()
        tiles(FOLLOW, as_sem.at[2]).wait()

    @pl.when(jnp.logical_not(collects))
    def _():
        tiles(len(LINE), as_sem.at[0]).wait()


def body(sizes, state, fx, fc, pw, cpl, modes, stiff, index, count, owner, shift):
    n_space, n_inst, n_blade = sizes
    half = n_inst // 2
    assert sizes == (SUB["zhi"] * SUB["x"], SUB["y"], SUB["zlo"] * SUB["core"])
    vmem = pl.BlockSpec(memory_space=pltpu.VMEM)
    hbm = pl.BlockSpec(memory_space=pltpu.HBM)
    dma = pltpu.SemaphoreType.DMA
    operands = (
        state.reshape(DEEP, NC),
        fx,
        fc,
        pw,
        cpl,
        modes.reshape(MODES, ROWS),
        stiff.reshape(1, MODES),
        index,
        owner,
        shift,
    )
    out, field, gain = pl.pallas_call(
        functools.partial(kernel, sizes),
        out_shape=(jax.ShapeDtypeStruct((DEEP, NC), F32), jax.ShapeDtypeStruct((HELD * CX, NC), F32), jax.ShapeDtypeStruct((COMP,), F32)),
        in_specs=[pl.BlockSpec(memory_space=pltpu.SMEM)] + [hbm] * len(operands),
        out_specs=(vmem, vmem, vmem),
        scratch_shapes=[
            pltpu.VMEM((DEEP, NC), jnp.bfloat16),
            pltpu.VMEM((2 * MODES, ROWS), F32),
            pltpu.SMEM((COMP, COMP), F32),
            pltpu.SMEM((COMP, COMP), F32),
            pltpu.SMEM((COMP,), F32),
            pltpu.VMEM((1, MODES), F32),
            pltpu.VMEM((1, ROWS), jnp.int32),
            pltpu.VMEM((1, ROWS), jnp.int32),
            pltpu.SMEM((n_blade * BPG,), jnp.int32),
            pltpu.VMEM((6 * MODES, ROWS), jnp.bfloat16),
            pltpu.VMEM((ROWS, LANES), jnp.bfloat16),
            pltpu.VMEM((DEEP, NC), F32),
            pltpu.VMEM((half, DEEP, NC), jnp.bfloat16),
            pltpu.VMEM((half, DEEP, NC), jnp.bfloat16),
            pltpu.VMEM((2, 16, NC), F32),
            pltpu.VMEM((2, 16, NC), jnp.bfloat16),
            pltpu.VMEM((2, 16, NC), jnp.bfloat16),
            pltpu.VMEM((CX * NB_LANE, HELD * LANES), F32),
            pltpu.VMEM((2, CX, LANES), F32),
            pltpu.VMEM(((FOLLOW + 1) * len(LINE) - 1, CX, LANES), F32),
            pltpu.VMEM((len(PLANE), CX, LANES), F32),
            pltpu.VMEM((CX, LANES), F32),
            dma((len(operands) + 1,)),
            dma((half, CHUNKS)),
            dma((half, CHUNKS)),
            dma((half, CHUNKS)),
            dma((half, CHUNKS)),
            dma((2,)),
            dma((2,)),
            dma((3,)),
            dma((3,)),
        ],
        compiler_params=pltpu.CompilerParams(
            collective_id=0, has_side_effects=True, vmem_limit_bytes=24 * 1024 * 1024
        ),
        name="residual",
    )(count, *[pltpu.with_memory_space_constraint(operand, pltpu.HBM) for operand in operands])
    wall = gain[None, :, None, None] * field.reshape(HELD, 1, CX, NC)
    return (out.reshape(HELD, COMP, CX, NC) + wall)[None]


def solution(mesh):
    sizes = (mesh.shape["space"], mesh.shape["inst"], mesh.shape["blade"])
    placed = (
        P("blade", "inst", None, "space", None),
        P(),
        P(),
        P(),
        P(),
        P("blade", None, "space"),
        P(),
        P("blade", "space"),
        P("blade", "space"),
        P("blade", "space"),
        P(),
    )
    return jax.shard_map(
        functools.partial(body, sizes),
        mesh=mesh,
        in_specs=placed,
        out_specs=P("blade", "inst", None, "space", None),
        check_vma=False,
    )
```

```python
import functools
import itertools
import math

import jax
import jax.numpy as jnp
from jax import lax
from jax.experimental import pallas as pl
from jax.experimental.pallas import tpu as pltpu
from jax.sharding import PartitionSpec as P

COMP = 5
CX = 8
NC = 1024
MODES = 64
ROWS = 256
BPG = 2
HELD = 2
PLANES = HELD * COMP
DEEP = PLANES * CX
LANES = 128
NB_LANE = NC // LANES
CHUNKS = 4
WIDTH = NC // CHUNKS
EARLY = 3


HIGH = lax.Precision.HIGHEST
MESH = pl.DeviceIdType.MESH
LOGICAL = pl.DeviceIdType.LOGICAL
F32 = jnp.float32


def spectral(offset, count):
    offset %= count
    if offset == 0:
        return 0.0
    angle = math.pi * offset / count
    return 0.5 * (-1.0) ** offset * math.cos(angle) / math.sin(angle)


def dot(a, b, dims):
    return lax.dot_general(a, b, (dims, ((), ())), precision=HIGH, preferred_element_type=F32)


SUB = {"zhi": 3, "x": 4, "y": 8, "zlo": 4, "core": 2}


STEP = {"core": 1, "zlo": 2, "y": 8, "x": 64, "zhi": 256}


def around(offset, size):
    return min(offset, size - offset)


LINE = list(itertools.product(range(SUB["zlo"]), range(SUB["core"])))
PLANE = sorted(
    (o for o in itertools.product(range(SUB["x"]), range(SUB["y"])) if any(o)),
    key=lambda o: -around(o[0], SUB["x"]) - around(o[1], SUB["y"]),
)
FOLLOW = SUB["zhi"] - 1


def place(space, inst, blade):
    here = {
        "zhi": space // SUB["x"],
        "x": space % SUB["x"],
        "y": inst,
        "zlo": blade // SUB["core"],
        "core": blade % SUB["core"],
    }
    table = {}
    for axis, size in SUB.items():
        table[axis] = []
        for offset in range(size):
            at = here[axis] + offset
            table[axis].append(jnp.where(at >= size, at - size, at) * STEP[axis])
    return here, table


def parts(values):
    upper = values.astype(jnp.bfloat16)
    return upper, (values - upper.astype(F32)).astype(jnp.bfloat16)


def kernel(
    sizes,
    count,
    state_hbm,
    fx_hbm,
    fc_hbm,
    pw_hbm,
    cpl_hbm,
    modes_hbm,
    stiff_hbm,
    index_hbm,
    owner_hbm,
    shift_hbm,
    out,
    field,
    gain,
    mine,
    phi,
    fx,
    fc,
    pw,
    stiff,
    index,
    owner,
    shift,
    phis,
    low_rows,
    dcs,
    fromleft,
    fromright,
    hrow,
    hsend,
    hrecv,
    pf,
    part,
    box0,
    box1,
    whole,
    load_sem,
    sl_sem,
    rl_sem,
    sr_sem,
    rr_sem,
    hs_sem,
    hr_sem,
    as_sem,
    ar_sem,
):
    n_space, n_inst, n_blade = sizes
    half = n_inst // 2
    ninst = n_inst * HELD
    my_space = lax.axis_index("space")
    my_inst = lax.axis_index("inst")
    my_blade = lax.axis_index("blade")

    moves = (
        (state_hbm, mine),
        (index_hbm, index),
        (pw_hbm, pw),
        (owner_hbm, owner),
        (shift_hbm, shift),
        (modes_hbm, phi.at[pl.ds(0, MODES)]),
        (modes_hbm, phi.at[pl.ds(MODES, MODES)]),
        (fx_hbm, fx),
        (fc_hbm, fc),
        (stiff_hbm, stiff),
        (cpl_hbm, gain),
    )
    loads = [pltpu.make_async_copy(src, dst, load_sem.at[n]) for n, (src, dst) in enumerate(moves)]
    for copy in loads:
        copy.start()

    here, table = place(my_space, my_inst, my_blade)
    column = table["x"][0] + table["y"][0]
    stack = table["zlo"][0] + table["core"][0]
    collects = here["zhi"] == 0

    def on_line(zhi, offsets):
        return column + zhi * STEP["zhi"] + table["zlo"][offsets[0]] + table["core"][offsets[1]]

    def on_plane(offsets):
        return stack + table["x"][offsets[0]] + table["y"][offsets[1]]

    right = lax.rem(my_inst + 1, n_inst)
    left = lax.rem(my_inst + n_inst - 1, n_inst)
    following = lax.rem(my_space + 1, n_space)
    preceding = lax.rem(my_space + n_space - 1, n_space)

    barrier = pltpu.get_barrier_semaphore()

    def greet(other):
        pl.semaphore_signal(barrier, inc=1, device_id=other, device_id_type=LOGICAL)

    first_x, last_x = here["x"] == 0, here["x"] == SUB["x"] - 1
    first_block, last_block = my_space == 0, my_space == n_space - 1
    up_step = last_x & (here["zhi"] < FOLLOW)

    def greet_space(other):
        pl.semaphore_signal(barrier, inc=1, device_id={"space": other}, device_id_type=MESH)

    for other in (left, right):
        pl.semaphore_signal(barrier, inc=1, device_id={"inst": other}, device_id_type=MESH)
    pl.when(jnp.logical_not(first_x))(lambda: greet_space(preceding))
    pl.when(jnp.logical_not(last_block))(lambda: greet_space(following))
    sides = jnp.where(first_block | last_x, 1, 2)

    @pl.when(collects)
    def _():
        for offsets in PLANE:
            greet(on_plane(offsets))
        for offsets in LINE[1:]:
            greet(on_line(0, offsets))
        for zhi in range(1, FOLLOW + 1):
            for offsets in LINE:
                greet(on_line(zhi, offsets))

    def columns(chunk):
        return pl.ds(chunk * WIDTH, WIDTH)

    def to_right(hop, chunk):
        src = mine if hop == 1 else fromleft.at[hop - 2]
        return pltpu.make_async_remote_copy(
            src_ref=src.at[:, columns(chunk)],
            dst_ref=fromleft.at[hop - 1, :, columns(chunk)],
            send_sem=sr_sem.at[hop - 1, chunk],
            recv_sem=rl_sem.at[hop - 1, chunk],
            device_id={"inst": right},
            device_id_type=MESH,
        )

    def to_left(hop, chunk):
        src = mine if hop == 1 else fromright.at[hop - 2]
        return pltpu.make_async_remote_copy(
            src_ref=src.at[:, columns(chunk)],
            dst_ref=fromright.at[hop - 1, :, columns(chunk)],
            send_sem=sl_sem.at[hop - 1, chunk],
            recv_sem=rr_sem.at[hop - 1, chunk],
            device_id={"inst": left},
            device_id_type=MESH,
        )

    def going(hop):
        rights = [c for c in range(CHUNKS) if hop < half or c < CHUNKS // 2]
        lefts = [c for c in reversed(range(CHUNKS)) if hop < half or c >= CHUNKS // 2]
        return list(zip(rights, lefts))

    def block(ref, lanes):
        got = []
        for group in range(DEEP // 16):
            pair = ref[pl.ds(16 * group, 16), lanes].astype(F32)
            got += [pair[0:CX], pair[CX : 2 * CX]]
        return got

    def lane_block(j):
        return pl.ds(pl.multiple_of(j * LANES, LANES), LANES)

    for copy in loads[0:5]:
        copy.wait()

    def pressure(j, carry):
        planes = block(mine, lane_block(j))
        for i in range(HELD):
            total = pw[0] * planes[i * COMP]
            for k in range(1, COMP):
                total = total + pw[k] * planes[i * COMP + k]
            pf[pl.ds(pl.multiple_of(j * CX, CX), CX), pl.ds(i * LANES, LANES)] = total
        return carry

    lax.fori_loop(0, NB_LANE, pressure, 0)

    cell = index[...]
    high = ((cell >> 7) & 7) * CX + (cell >> 10)
    low = cell & (LANES - 1)
    at_high = (lax.broadcasted_iota(jnp.int32, (CX * NB_LANE, ROWS), 0) == high).astype(F32)
    at_low = lax.broadcasted_iota(jnp.int32, (LANES, ROWS), 0) == low
    live = lax.broadcasted_iota(jnp.int32, (1, ROWS), 1) < count[0, 0]
    lag = jnp.where(owner[...] == 0, shift[my_blade * BPG], shift[my_blade * BPG + 1])
    slot = lax.broadcasted_iota(jnp.int32, (ninst, ROWS), 0)
    picks = [(((my_inst * HELD + i - lag) & (ninst - 1)) == slot) & live for i in range(HELD)]

    rows = dot(pf[...], at_high, ((0,), (0,)))
    placed = jnp.zeros((ninst, ROWS), F32)
    for i in range(HELD):
        prow = jnp.sum(jnp.where(at_low, rows[i * LANES : (i + 1) * LANES], 0.0), axis=0, keepdims=True)
        placed = placed + jnp.where(picks[i], prow, 0.0)
    for copy in loads[5:7]:
        copy.wait()
    force = dot(placed, phi[...], ((1,), (1,)))
    first_half = lax.broadcasted_iota(jnp.int32, (CX, LANES), 1) < MODES
    part[0] = jnp.where(first_half, force[0:CX], force[CX : 2 * CX])

    def tile(src, dst, stage, other):
        return pltpu.make_async_remote_copy(
            src_ref=src,
            dst_ref=dst,
            send_sem=as_sem.at[stage],
            recv_sem=ar_sem.at[stage],
            device_id=other,
            device_id_type=LOGICAL,
        )

    def tiles(number, sem):
        some = box1.at[pl.ds(0, number)]
        return pltpu.make_async_copy(some, some, sem)

    def sum_box(first, box, number, stage):
        pltpu.make_async_copy(box, box, ar_sem.at[stage]).wait()
        total = first
        for k in range(number):
            total = total + box[k]
        return total

    @pl.when(collects)
    def _():
        pl.semaphore_wait(barrier, 2 + len(PLANE) + len(LINE) - 1 + sides)

    @pl.when(jnp.logical_not(collects))
    def _():
        pl.semaphore_wait(barrier, 2 + len(LINE) + sides)
        for k, offsets in enumerate(LINE):
            tile(part.at[0], box0.at[(here["zhi"] - 1) * len(LINE) + k], 0, on_line(0, offsets)).start()

    for c_right, c_left in going(1):
        to_right(1, c_right).start()
        to_left(1, c_left).start()

    @pl.when(collects)
    def _():
        for k, offsets in enumerate(LINE[1:]):
            tile(part.at[0], box0.at[FOLLOW * len(LINE) + k], 0, on_line(0, offsets)).start()

    hrow[...] = jnp.zeros_like(hrow)
    for group in range(DEEP // 16):
        pair = mine[pl.ds(16 * group, 16), :].astype(F32)
        for odd in range(2):
            plane = 2 * group + odd
            hrow[0, pl.ds(plane, 1), :] = pair[odd * CX : odd * CX + 1]
            hrow[1, pl.ds(plane, 1), :] = pair[odd * CX + CX - 1 : odd * CX + CX]
    for side in range(2):
        hsend[side] = hrow[side].astype(jnp.bfloat16)
    halos = []
    for side, other in ((0, preceding), (1, following)):
        halos.append(
            pltpu.make_async_remote_copy(
                src_ref=hsend.at[side],
                dst_ref=hrecv.at[side],
                send_sem=hs_sem.at[side],
                recv_sem=hr_sem.at[side],
                device_id={"space": other},
                device_id_type=MESH,
            )
        )

    pl.when(jnp.logical_not(first_block))(halos[0].start)
    pl.when(jnp.logical_not(last_block | up_step))(halos[1].start)

    upper, lower = parts(phi[...])
    for n, term in enumerate((upper, upper, lower)):
        phis[pl.ds(2 * MODES * n, 2 * MODES), :] = term
    low_rows[...] = jnp.where(at_low, 1.0, 0.0).T.astype(jnp.bfloat16)

    for group in range(DEEP // 16):
        pair = mine[pl.ds(16 * group, 16), :].astype(F32)
        ahead = pltpu.roll(pair, NC - 1, 1)
        behind = pltpu.roll(pair, 1, 1)
        dcs[pl.ds(16 * group, 16), :] = ahead - behind
        out[pl.ds(16 * group, 16), :] = pair - 0.25 * (ahead + behind)

    def receive(hop, first=0, last=None):
        onward = going(hop + 1) if hop < half else []
        for pair in going(hop)[first:last]:
            to_right(hop, pair[0]).wait_recv()
            if pair[0] in [c for c, _ in onward]:
                to_right(hop + 1, pair[0]).start()
            to_left(hop, pair[1]).wait_recv()
            if pair[1] in [c for _, c in onward]:
                to_left(hop + 1, pair[1]).start()

    receive(1)

    @pl.when(up_step)
    def _():
        halos[0].wait_recv()
        halos[1].start()

    receive(2, 0, EARLY)

    @pl.when(collects)
    def _():
        part[1] = sum_box(part[0], box0, (FOLLOW + 1) * len(LINE) - 1, 0)
        for k, offsets in enumerate(PLANE):
            tile(part.at[1], box1.at[k], 1, on_plane(offsets)).start()

    layer = lax.broadcasted_iota(jnp.int32, (CX, LANES), 0)

    def local(j, carry):
        lanes = lane_block(j)
        planes = block(mine, lanes)
        for i in range(HELD):
            dx, dc = [], []
            for k in range(COMP):
                p = i * COMP + k
                up = jnp.where(layer == CX - 1, hrow[0, pl.ds(p, 1), lanes], pltpu.roll(planes[p], CX - 1, 0))
                down = jnp.where(layer == 0, hrow[1, pl.ds(p, 1), lanes], pltpu.roll(planes[p], 1, 0))
                dx.append(up - down)
                dc.append(dcs[pl.ds(p * CX, CX), lanes])
                at = pl.ds(p * CX, CX)
                value = out[at, lanes] - 0.25 * (up + down)
                for r in range(HELD):
                    value = value + spectral(i - r, ninst) * planes[r * COMP + k]
                out[at, lanes] = value
            for k in range(COMP):
                at = pl.ds((i * COMP + k) * CX, CX)
                flow = fx[k, 0] * dx[0] + fc[k, 0] * dc[0]
                for c in range(1, COMP):
                    flow = flow + fx[k, c] * dx[c] + fc[k, c] * dc[c]
                out[at, lanes] = out[at, lanes] + 0.5 * flow
        return carry

    def add_blocks(sources, first, last):
        def add(j, carry):
            lanes = lane_block(j)
            sums = [out[pl.ds(p * CX, CX), lanes] for p in range(PLANES)]
            for ref, offset in sources:
                planes = block(ref, lanes)
                for i in range(HELD):
                    for k in range(COMP):
                        for r in range(HELD):
                            sums[i * COMP + k] += spectral(HELD * offset + i - r, ninst) * planes[r * COMP + k]
            for p in range(PLANES):
                out[pl.ds(p * CX, CX), lanes] = sums[p]
            return carry

        lax.fori_loop(first, last, add, 0)

    for hop in range(1, half):
        if hop > 1:
            receive(hop, EARLY if hop == 2 else 0)
        add_blocks([(fromleft.at[hop - 1], hop), (fromright.at[hop - 1], -hop)], 0, NB_LANE)

    for copy in loads[7:]:
        copy.wait()
    pl.when(jnp.logical_not(last_block | up_step))(halos[0].wait_recv)
    pl.when(jnp.logical_not(first_block))(halos[1].wait_recv)

    def neighbour(side, end):
        @pl.when(end)
        def _():
            hrow[side] = jnp.zeros((16, NC), F32)

        @pl.when(jnp.logical_not(end))
        def _():
            hrow[side] = hrecv[side].astype(F32)

    neighbour(0, last_block)
    neighbour(1, first_block)
    lax.fori_loop(0, NB_LANE, local, 0)

    @pl.when(collects)
    def _():
        whole[...] = sum_box(part[1], box1, len(PLANE), 1)
        for zhi in range(1, FOLLOW + 1):
            tile(whole, whole, 2, on_line(zhi, LINE[0])).start()

    receive(half)
    add_blocks([(fromleft.at[half - 1], half)], 0, NB_LANE // 2)
    add_blocks([(fromright.at[half - 1], -half)], NB_LANE // 2, NB_LANE)

    @pl.when(jnp.logical_not(collects))
    def _():
        pltpu.make_async_copy(whole, whole, ar_sem.at[2]).wait()

    total = whole[...]
    rigid = jnp.concatenate([stiff[...], stiff[...]], axis=1)
    amp = total / rigid
    both = jnp.concatenate([jnp.where(first_half, amp, 0.0), jnp.where(first_half, 0.0, amp)], axis=0)
    upper, lower = parts(both)
    moved = jnp.dot(jnp.concatenate([upper, lower, upper], axis=1), phis[...], preferred_element_type=F32)
    spread = []
    for i in range(HELD):
        disp = jnp.sum(jnp.where(picks[i], moved, 0.0), axis=0, keepdims=True)
        spread.append(at_high * disp)
    upper, lower = parts(jnp.concatenate(spread, axis=0))
    hits = [jnp.dot(term, low_rows[...], preferred_element_type=F32) for term in (upper, lower)]
    hit = hits[0] + hits[1]
    for i in range(HELD):
        for j in range(NB_LANE):
            at = (i * NB_LANE + j) * CX
            field[pl.ds(i * CX, CX), pl.ds(j * LANES, LANES)] = hit[at : at + CX]

    for hop in range(1, half + 1):
        for c_right, c_left in going(hop):
            to_right(hop, c_right).wait_send()
            to_left(hop, c_left).wait_send()
    pl.when(jnp.logical_not(first_block))(halos[0].wait_send)
    pl.when(jnp.logical_not(last_block))(halos[1].wait_send)

    @pl.when(collects)
    def _():
        tiles(len(LINE) - 1, as_sem.at[0]).wait()
        tiles(len(PLANE), as_sem.at[1]).wait()
        tiles(FOLLOW, as_sem.at[2]).wait()

    @pl.when(jnp.logical_not(collects))
    def _():
        tiles(len(LINE), as_sem.at[0]).wait()


def body(sizes, state, fx, fc, pw, cpl, modes, stiff, index, count, owner, shift):
    n_space, n_inst, n_blade = sizes
    half = n_inst // 2
    assert sizes == (SUB["zhi"] * SUB["x"], SUB["y"], SUB["zlo"] * SUB["core"])
    vmem = pl.BlockSpec(memory_space=pltpu.VMEM)
    hbm = pl.BlockSpec(memory_space=pltpu.HBM)
    dma = pltpu.SemaphoreType.DMA
    operands = (
        state.reshape(DEEP, NC),
        fx,
        fc,
        pw,
        cpl,
        modes.reshape(MODES, ROWS),
        stiff.reshape(1, MODES),
        index,
        owner,
        shift,
    )
    out, field, gain = pl.pallas_call(
        functools.partial(kernel, sizes),
        out_shape=(jax.ShapeDtypeStruct((DEEP, NC), F32), jax.ShapeDtypeStruct((HELD * CX, NC), F32), jax.ShapeDtypeStruct((COMP,), F32)),
        in_specs=[pl.BlockSpec(memory_space=pltpu.SMEM)] + [hbm] * len(operands),
        out_specs=(vmem, vmem, vmem),
        scratch_shapes=[
            pltpu.VMEM((DEEP, NC), jnp.bfloat16),
            pltpu.VMEM((2 * MODES, ROWS), F32),
            pltpu.SMEM((COMP, COMP), F32),
            pltpu.SMEM((COMP, COMP), F32),
            pltpu.SMEM((COMP,), F32),
            pltpu.VMEM((1, MODES), F32),
            pltpu.VMEM((1, ROWS), jnp.int32),
            pltpu.VMEM((1, ROWS), jnp.int32),
            pltpu.SMEM((n_blade * BPG,), jnp.int32),
            pltpu.VMEM((6 * MODES, ROWS), jnp.bfloat16),
            pltpu.VMEM((ROWS, LANES), jnp.bfloat16),
            pltpu.VMEM((DEEP, NC), F32),
            pltpu.VMEM((half, DEEP, NC), jnp.bfloat16),
            pltpu.VMEM((half, DEEP, NC), jnp.bfloat16),
            pltpu.VMEM((2, 16, NC), F32),
            pltpu.VMEM((2, 16, NC), jnp.bfloat16),
            pltpu.VMEM((2, 16, NC), jnp.bfloat16),
            pltpu.VMEM((CX * NB_LANE, HELD * LANES), F32),
            pltpu.VMEM((2, CX, LANES), F32),
            pltpu.VMEM(((FOLLOW + 1) * len(LINE) - 1, CX, LANES), F32),
            pltpu.VMEM((len(PLANE), CX, LANES), F32),
            pltpu.VMEM((CX, LANES), F32),
            dma((len(operands) + 1,)),
            dma((half, CHUNKS)),
            dma((half, CHUNKS)),
            dma((half, CHUNKS)),
            dma((half, CHUNKS)),
            dma((2,)),
            dma((2,)),
            dma((3,)),
            dma((3,)),
        ],
        compiler_params=pltpu.CompilerParams(
            collective_id=0, has_side_effects=True, vmem_limit_bytes=24 * 1024 * 1024
        ),
        name="residual",
    )(count, *[pltpu.with_memory_space_constraint(operand, pltpu.HBM) for operand in operands])
    wall = gain[None, :, None, None] * field.reshape(HELD, 1, CX, NC)
    return (out.reshape(HELD, COMP, CX, NC) + wall)[None]


def solution(mesh):
    sizes = (mesh.shape["space"], mesh.shape["inst"], mesh.shape["blade"])
    placed = (
        P("blade", "inst", None, "space", None),
        P(),
        P(),
        P(),
        P(),
        P("blade", None, "space"),
        P(),
        P("blade", "space"),
        P("blade", "space"),
        P("blade", "space"),
        P(),
    )
    return jax.shard_map(
        functools.partial(body, sizes),
        mesh=mesh,
        in_specs=placed,
        out_specs=P("blade", "inst", None, "space", None),
        check_vma=False,
    )
```
